256 devices in a mesh: docs: 8 (over x, z_lo), cent: 32 (over z_hi, y, core).
Axes of the slice: x: 4, y: 4, z: 8 (z_hi: 4, z_lo: 2; z = z_hi * 2 + z_lo), core: 2. Of those that a mesh axis runs over, the one named last changes fastest.
Arguments:
- loader_blocks: bfloat16 [8, 32, 512, 384], P('docs', 'cent'), may hold values from -6 to 6
- block_counts: int32 [8, 32], P('docs', 'cent'), may hold values from 1 to 4, 64 in all within a row
- block_dest: int32 [8, 64], P('docs'), may hold values from 0 to 63, each once within a row
- centroids: bfloat16 [384, 16384], P(None, 'cent'), may hold values from -0.3125 to 0.3125
Outputs:
- centroid_sums: float32 [384, 16384], P('docs', 'cent')
- doc_weights: float32 [65536], P('docs')
The draws below stay inside these ranges and needn't reach their ends.
Inputs may be any that keep to these rules, and one draw needn't show every extreme that they name: `block_counts`: each row sums to 64; every row has a host with exactly 4 live blocks. `block_dest`: each row is a permutation of 0 to 63.
All inputs are finite; a program needn't handle non-finite values.
Results may differ from the reference program's by a relative error of at most 0.0007.
The reference program's roundings to bfloat16 on the way count: a program that leaves them out, or rounds other values in their place, can miss the bound.
Values may be sent and summed in bfloat16 or wider, within the bound.
A program may use at most 64 MiB of HBM per device.

```python
import math
import jax
import jax.numpy as jnp
import numpy as np
from jax import lax

D = 384
CENTROIDS = 16384
ROWS_DEV = 8192
ROW_BLOCK = 128
ITERS = 2
SCORE_ROWS = 1024
BLOCKS = 64
MOST = 4
SLOT_ROWS = 512
DOCS = 65536
N_DOCS = 8
N_CENT = 32


def block_levels(own_key, dims, pieces, smallest, high):
    gain, own = 1.0, jax.random.fold_in(own_key, 6)
    for axis_at, shards_of in pieces:
        steps = jnp.exp(jax.random.uniform(jax.random.fold_in(own, axis_at), (shards_of,), jnp.float32, smallest / len(pieces), high / len(pieces)))
        gain = gain * jnp.repeat(steps, dims[axis_at] // shards_of).reshape([-1 if axis == axis_at else 1 for axis in range(len(dims))])
    return gain


def profile(number_of, total, reach, slope):
    weights = [(1 << 20) // math.isqrt(standing ** slope) + 1 for standing in range(2, number_of + 1)]
    spare, holding = total - reach - (number_of - 1), [1] * (number_of - 1)
    while spare > 0:
        free = [i for i in range(number_of - 1) if holding[i] < reach]
        whole, left = sum([weights[i] for i in free]), spare
        for i in free:
            extra = min(reach - holding[i], max(1, left * weights[i] // whole), spare)
            holding[i] = holding[i] + extra
            spare = spare - extra
    return np.array([reach] + holding)


def ragged_sizes(own_key, number_of, total, reach, slope):
    if number_of == 2:
        one = jax.random.randint(own_key, (), max(1, total - reach), min(reach, total - 1) + 1)
        return jnp.stack([one, total - one])
    lengths = jnp.asarray(profile(number_of, total, reach, slope), jnp.int32)
    pairs = (number_of - 1) // 2
    donor, sink = lengths[1:1 + 2 * pairs:2], lengths[2:2 + 2 * pairs:2]
    margin = jnp.minimum(donor - 1, reach - sink)
    passed = jax.random.randint(jax.random.fold_in(own_key, 1), (pairs,), 0, 1 << 20) % (margin + 1)
    lengths = lengths.at[1:1 + 2 * pairs:2].set(donor - passed).at[2:2 + 2 * pairs:2].set(sink + passed)
    return lengths[jax.random.permutation(jax.random.fold_in(own_key, 2), number_of)]


def bell_draw(rng, shape, spread, limit, split=(), kind=jnp.bfloat16):
    array = spread * jax.random.normal(rng, shape, jnp.float32)
    if split:
        array = array * block_levels(rng, shape, split, -0.22, 0.18)
    return jnp.clip(array, -limit, limit).astype(kind)


def setup_inputs(seed: int = 0) -> dict:
    keys = jax.random.split(jax.random.key(seed), 5)
    loader_blocks = bell_draw(keys[0], (N_DOCS, N_CENT, SLOT_ROWS, D), 1.0, 6.0, ((0, 8), (1, 32)))
    block_counts = jax.vmap(lambda own: ragged_sizes(own, N_CENT, BLOCKS, MOST, 2))(jax.random.split(keys[1], N_DOCS)).reshape((N_DOCS, N_CENT)).astype(jnp.int32)
    block_dest = jax.vmap(lambda own: jax.random.permutation(own, BLOCKS))(jax.random.split(keys[2], N_DOCS)).reshape((N_DOCS, BLOCKS)).astype(jnp.int32)
    centroids = bell_draw(keys[3], (D, CENTROIDS), D ** -0.5, 0.3125, ((1, 32),))
    return {"loader_blocks": loader_blocks, "block_counts": block_counts, "block_dest": block_dest, "centroids": centroids}


SHARPNESS = 25.0

def unit_rows(rows):
    values = rows.astype(jnp.float32)
    factor = lax.rsqrt(lax.optimization_barrier(jnp.mean(values * values, axis=-1, keepdims=True)) + 1e-06)
    return (values * factor * values.shape[-1] ** (-0.5)).astype(jnp.bfloat16)

def unit_columns(weights):
    values = weights.astype(jnp.float32)
    factor = lax.rsqrt(lax.optimization_barrier(jnp.mean(values * values, axis=0, keepdims=True)) + 1e-06)
    return (values * factor * values.shape[0] ** (-0.5)).astype(jnp.bfloat16)

def invert_order(dest):
    count = dest.shape[0]
    where_p = jnp.arange(count, dtype=jnp.int32)
    return lax.optimization_barrier(jnp.sum(jnp.where(dest[None, :] == where_p[:, None], where_p[None, :], 0), axis=1)).astype(jnp.int32)

def source_slots(counts, dest, most):
    hosts = counts.shape[0]
    starts = (jnp.cumsum(counts) - counts).astype(jnp.int32)
    inverse = invert_order(dest)
    owner = lax.optimization_barrier(jnp.sum((starts[None, :] <= inverse[:, None]).astype(jnp.int32), axis=1)) - 1
    host_ids = jnp.arange(hosts, dtype=jnp.int32)
    begin = lax.optimization_barrier(jnp.sum(jnp.where(host_ids[None, :] == owner[:, None], starts[None, :], 0), axis=1))
    return (owner * most + (inverse - begin)).astype(jnp.int32)

def reference(loader_blocks, block_counts, block_dest, centroids):
    groups = []
    for group in range(N_DOCS):
        flat = source_slots(block_counts[group], block_dest[group], MOST)
        pool = loader_blocks[group].reshape(-1, ROW_BLOCK, D)
        groups.append(pool[flat].reshape(ROWS_DEV, D))
    unit_docs = unit_rows(jnp.concatenate(groups, axis=0))
    unit_cents = unit_columns(centroids)
    tiles = unit_docs.reshape(DOCS // SCORE_ROWS, SCORE_ROWS, D)

    def kernel(tile):
        return jnp.exp(SHARPNESS * jnp.dot(tile, unit_cents, preferred_element_type=jnp.float32))

    def first_step(carry, tile):
        return (carry + lax.optimization_barrier(jnp.sum(kernel(tile), axis=0)), None)
    column_sum, _ = lax.scan(first_step, jnp.zeros((CENTROIDS,), jnp.float32), tiles)
    cent_scale = 1.0 / (CENTROIDS * column_sum)
    for turn in range(ITERS):

        def sweep(carry, tile):
            weights = kernel(tile)
            row_sum = lax.optimization_barrier(jnp.sum(weights * cent_scale[None, :], axis=1))
            doc_scale = 1.0 / (DOCS * row_sum)
            return (carry + lax.optimization_barrier(jnp.sum(doc_scale[:, None] * weights, axis=0)), None)
        if turn + 1 < ITERS:
            column_sum, _ = lax.scan(sweep, jnp.zeros((CENTROIDS,), jnp.float32), tiles)
            cent_scale = 1.0 / (CENTROIDS * column_sum)
        else:

            def final(carry, tile):
                weights = kernel(tile)
                row_sum = lax.optimization_barrier(jnp.sum(weights * cent_scale[None, :], axis=1))
                doc_scale = 1.0 / (DOCS * row_sum)
                plan = (DOCS * doc_scale[:, None] * weights * cent_scale[None, :]).astype(jnp.bfloat16)
                term = lax.dot_general(tile, plan, (((0,), (0,)), ((), ())), preferred_element_type=jnp.float32)
                return (carry + term, doc_scale)
            sums, scales = lax.scan(final, jnp.zeros((D, CENTROIDS), jnp.float32), tiles)
    doc_weights = jnp.log(DOCS * scales.reshape(DOCS))
    return (sums, doc_weights)
```

```python
import jax
import jax.numpy as jnp
from jax import lax
from jax.experimental import pallas as pl
from jax.experimental.pallas import tpu as pltpu
from jax.sharding import PartitionSpec as P

F32 = jnp.float32
BF16 = jnp.bfloat16

WIDTH = 384
COLS = 512
SLOTS = 512
BLOCK = 128
MOST = 4
HOSTS = 8
BLOCKS = HOSTS * MOST
QUARTERS = 4
SHARPNESS = 25.0
DOCS = 65536.0
CENTROIDS = 16384.0


def mod(value, size):
    return lax.rem(value, jnp.int32(size))


def wide(tile):
    return jnp.concatenate([tile] * (COLS // BLOCK), axis=1)


def device(x, y, z, core):
    return (x * 2 + mod(z, 2), (lax.div(z, jnp.int32(2)) * 4 + y) * 2 + core)


def kernel(
    docs_ref,
    counts_ref,
    dest_ref,
    cents_ref,
    numer_out,
    weights_out,
    units,
    units_t,
    cents,
    score,
    live_counts,
    live,
    col_acc,
    col_x,
    col_z,
    scale,
    rows,
    doc_row,
    doc_col,
    numer,
    far,
    near,
    reduced,
    shares,
    doc_log,
    unit_send,
    unit_recv,
    cent_send,
    cent_recv,
    count_send,
    count_recv,
    colx_send,
    colx_recv,
    colz_send,
    colz_recv,
    row_send,
    row_recv,
    log_send,
    log_recv,
    sum_send,
    sum_recv,
    share_send,
    share_recv,
):
    doc_index = lax.axis_index("docs")
    cent_index = lax.axis_index("cent")
    x = lax.div(doc_index, jnp.int32(2))
    lo = mod(doc_index, 2)
    core = mod(cent_index, 2)
    y = mod(lax.div(cent_index, jnp.int32(2)), 4)
    hi = lax.div(cent_index, jnp.int32(8))
    z = hi * 2 + lo
    host = y * 2 + core

    def along_host(step):
        other = mod(host + step, HOSTS)
        return device(x, lax.div(other, jnp.int32(2)), z, mod(other, 2))

    def along_x(step):
        return device(mod(x + step, 4), y, z, core)

    def along_z(step):
        return device(x, y, mod(z + step, 8), core)

    def along_y(step):
        return device(x, mod(y + step, 4), z, core)

    def remote(src, dst, send, recv, target):
        return pltpu.make_async_remote_copy(
            src_ref=src,
            dst_ref=dst,
            send_sem=send,
            recv_sem=recv,
            device_id=target,
            device_id_type=pl.DeviceIdType.MESH,
        )

    barrier = pltpu.get_barrier_semaphore()
    for step in range(1, 8):
        pl.semaphore_signal(
            barrier, inc=1, device_id=along_host(step), device_id_type=pl.DeviceIdType.MESH
        )
        pl.semaphore_signal(
            barrier, inc=1, device_id=along_z(step), device_id_type=pl.DeviceIdType.MESH
        )
    for step in range(1, 4):
        pl.semaphore_signal(
            barrier, inc=1, device_id=along_x(step), device_id_type=pl.DeviceIdType.MESH
        )

    values = docs_ref[...].astype(F32)
    factor = lax.rsqrt(jnp.mean(values * values, axis=1, keepdims=True) + 1e-06)
    units[host] = (values * factor * WIDTH ** (-0.5)).astype(BF16)
    values = cents_ref[...].astype(F32)
    factor = lax.rsqrt(jnp.mean(values * values, axis=0, keepdims=True) + 1e-06)
    cents[hi] = (values * factor * WIDTH ** (-0.5)).astype(BF16)
    live_counts[host] = jnp.full((8, BLOCK), counts_ref[0, 0].astype(F32), F32)
    col_acc[...] = jnp.zeros_like(col_acc)

    pl.semaphore_wait(barrier, 17)

    left_y, right_y, far_y = mod(y + 3, 4), mod(y + 1, 4), mod(y + 2, 4)
    first, second, whole = pl.ds(0, SLOTS // 2), pl.ds(SLOTS // 2, SLOTS // 2), pl.ds(0, SLOTS)
    to_right, to_left = along_y(1), along_y(3)
    to_twin = device(x, y, z, 1 - core)
    own, from_left, from_right, across = (
        host,
        left_y * 2 + core,
        right_y * 2 + core,
        far_y * 2 + core,
    )
    unit_plan = [
        (own, first, to_right),
        (own, second, to_right),
        (own, first, to_left),
        (own, second, to_left),
        (from_left, first, to_right),
        (from_right, second, to_left),
        (own, whole, to_twin),
        (from_left, first, to_twin),
        (from_left, second, to_twin),
        (from_right, first, to_twin),
        (from_right, second, to_twin),
        (across, first, to_twin),
        (across, second, to_twin),
    ]
    unit_copies = []
    for at, (which, part, target) in enumerate(unit_plan):
        ref = units.at[which, part]
        unit_copies.append(remote(ref, ref, unit_send.at[at], unit_recv.at[at], target))

    chunk = WIDTH // 4
    rising, falling = [], []
    for step in range(6):
        back = 1 if step < 4 else 2
        which = mod(hi - back + lo + 4, QUARTERS)
        ref = cents.at[which, pl.ds((step % 4) * chunk, chunk)]
        rising.append(remote(ref, ref, cent_send.at[step], cent_recv.at[step], along_z(1)))
        ahead = 0 if step < 4 else 1
        which = mod(hi + ahead + lo, QUARTERS)
        ref = cents.at[which, pl.ds(((step + 2) % 4) * chunk, chunk)]
        falling.append(
            remote(ref, ref, cent_send.at[6 + step], cent_recv.at[6 + step], along_z(7))
        )

    def cent_open():
        @pl.when(lo == 1)
        def _():
            for step in range(4):
                rising[step].start()

        @pl.when(lo == 0)
        def _():
            for step in range(4):
                falling[step].start()

    def cent_start(step):
        @pl.when(lo == 1)
        def _():
            if step >= 4:
                rising[step - 4].wait_recv()
                rising[step].start()
            falling[step].wait_recv()
            falling[step].start()

        @pl.when(lo == 0)
        def _():
            if step >= 4:
                falling[step - 4].wait_recv()
                falling[step].start()
            rising[step].wait_recv()
            rising[step].start()

    def cent_finish():
        @pl.when(lo == 1)
        def _():
            for step in range(2, 6):
                rising[step].wait_recv()

        @pl.when(lo == 0)
        def _():
            for step in range(2, 6):
                falling[step].wait_recv()

    count_copies = [
        remote(
            live_counts.at[host],
            live_counts.at[host],
            count_send.at[step - 1],
            count_recv.at[step - 1],
            along_host(step),
        )
        for step in range(1, 8)
    ]
    for at in (0, 3, 1, 2, 6):
        unit_copies[at].start()
    for copy in count_copies:
        copy.start()
    cent_open()

    def score_tile(turn_y, flip, turn_z):
        which = mod(y + (turn_y ^ (turn_y >> 1)), 4) * 2 + (core ^ flip)
        quarter = mod(hi + (turn_z ^ (turn_z >> 1)), QUARTERS)
        logits = jnp.dot(units[which], cents[quarter], preferred_element_type=F32)
        weights = jnp.exp(SHARPNESS * logits)
        score[quarter, pl.ds(pl.multiple_of(which * SLOTS, SLOTS), SLOTS), :] = weights
        total = col_acc[quarter]
        for slot in range(MOST):
            part = weights[slot * BLOCK : (slot + 1) * BLOCK]
            part = jnp.sum(part.reshape(BLOCK // 8, 8, COLS), axis=0)
            here = jnp.where(live_counts[which] > slot, 1.0, 0.0)
            total = total + part * wide(here)
        col_acc[quarter] = total

    def score_tiles(turns_y, turns_z):
        (y_from, y_to), (z_from, z_to) = turns_y, turns_z
        wide_z = z_to - z_from

        def body(at, _):
            turn_z = z_from + lax.rem(at, wide_z)
            rest = lax.div(at, wide_z)
            score_tile(y_from + (rest >> 1), rest & 1, turn_z)
            return 0

        lax.fori_loop(0, (y_to - y_from) * 2 * wide_z, body, 0)

    for copy in count_copies:
        copy.wait_recv()
    cent_start(0)
    unit_copies[0].wait_recv()
    unit_copies[4].start()
    unit_copies[7].start()
    unit_copies[3].wait_recv()
    unit_copies[5].start()
    unit_copies[10].start()
    cent_start(1)
    unit_copies[6].wait_recv()
    score_tiles((0, 1), (0, 1))
    cent_start(2)
    cent_start(3)
    for at in (1, 2):
        unit_copies[at].wait_recv()
    for at in (8, 9):
        unit_copies[at].start()
    cent_start(4)
    cent_start(5)
    for at in (7, 8, 9, 10):
        unit_copies[at].wait_recv()
    score_tiles((1, 3), (0, 1))
    for at in (4, 5):
        unit_copies[at].wait_recv()
    for at in (11, 12):
        unit_copies[at].start()
    cent_finish()
    score_tiles((0, 3), (1, 4))
    for at in (11, 12):
        unit_copies[at].wait_recv()
    score_tiles((3, 4), (0, 4))

    for at in range(13):
        unit_copies[at].wait_send()
    for step in range(6):
        rising[step].wait_send()
        falling[step].wait_send()
    for copy in count_copies:
        copy.wait_send()

    for which in range(HOSTS):
        units_t[which] = units[which].T
        for slot in range(MOST):
            at = which * MOST + slot
            live[at : at + 1, :] = jnp.where(live_counts[which, 0:1, :] > slot, 1.0, 0.0)

    def exchange_columns(turn):
        for quarter in range(QUARTERS):
            total = jnp.sum(col_acc[quarter], axis=0, keepdims=True)
            for part in range(2):
                col_x[turn, x, 2 * quarter + part : 2 * quarter + part + 1, :] = total[
                    :, part * 256 : (part + 1) * 256
                ]
        copies = [
            remote(
                col_x.at[turn, x],
                col_x.at[turn, x],
                colx_send.at[turn * 3 + step - 1],
                colx_recv.at[turn * 3 + step - 1],
                along_x(step),
            )
            for step in range(1, 4)
        ]
        for copy in copies:
            copy.start()
        for copy in copies:
            copy.wait()
        col_z[turn, z] = (col_x[turn, 0] + col_x[turn, 1]) + (col_x[turn, 2] + col_x[turn, 3])
        copies = [
            remote(
                col_z.at[turn, z],
                col_z.at[turn, z],
                colz_send.at[turn * 7 + step - 1],
                colz_recv.at[turn * 7 + step - 1],
                along_z(step),
            )
            for step in range(1, 8)
        ]
        for copy in copies:
            copy.start()
        for copy in copies:
            copy.wait()
        total = col_z[turn, 0]
        for other in range(1, 8):
            total = total + col_z[turn, other]
        result = 1.0 / (CENTROIDS * total)
        for quarter in range(QUARTERS):
            line = jnp.concatenate(
                [result[2 * quarter : 2 * quarter + 1], result[2 * quarter + 1 : 2 * quarter + 2]],
                axis=1,
            )
            scale[quarter] = jnp.broadcast_to(line, (8, COLS))

    def row_sums(turn):
        def body(at, _):
            total = None
            for quarter in range(QUARTERS):
                weights = score[quarter, pl.ds(pl.multiple_of(at * BLOCK, BLOCK), BLOCK), :]
                weights = weights.reshape(BLOCK // 8, 8, COLS) * scale[quarter][None]
                weights = weights.reshape(BLOCK, COLS)
                for part in range(COLS // BLOCK):
                    piece = weights[:, part * BLOCK : (part + 1) * BLOCK]
                    total = piece if total is None else total + piece
            rows[turn, host, pl.ds(at, 1), :] = jnp.sum(total.T, axis=0, keepdims=True)
            return 0

        lax.fori_loop(0, BLOCKS, body, 0)
        copies = [
            remote(
                rows.at[turn, host],
                rows.at[turn, host],
                row_send.at[turn * 7 + step - 1],
                row_recv.at[turn * 7 + step - 1],
                along_host(step),
            )
            for step in range(1, 8)
        ]
        for copy in copies:
            copy.start()
        for copy in copies:
            copy.wait()
        total = rows[turn, 0]
        for other in range(1, HOSTS):
            total = total + rows[turn, other]
        return 1.0 / (DOCS * total)

    exchange_columns(0)

    doc_row[...] = row_sums(0) * live[...]

    def column_body(at, sums):
        line = jnp.broadcast_to(doc_row[pl.ds(at, 1), :], (BLOCK, BLOCK)).T
        line = wide(line)
        out = []
        for quarter in range(QUARTERS):
            weights = score[quarter, pl.ds(pl.multiple_of(at * BLOCK, BLOCK), BLOCK), :] * line
            out.append(sums[quarter] + jnp.sum(weights.reshape(BLOCK // 8, 8, COLS), axis=0))
        return tuple(out)

    sums = lax.fori_loop(
        0, BLOCKS, column_body, tuple(jnp.zeros((8, COLS), F32) for _ in range(QUARTERS))
    )
    for quarter in range(QUARTERS):
        col_acc[quarter] = sums[quarter]
    exchange_columns(1)

    doc_scale = row_sums(1)
    doc_log[hi, 0:BLOCKS, :] = jnp.log(DOCS * doc_scale)
    for which in range(HOSTS):
        doc_log[hi, BLOCKS + which : BLOCKS + which + 1, :] = live_counts[which, 0:1, :]
    log_copies = [
        remote(
            doc_log.at[hi],
            doc_log.at[hi],
            log_send.at[step - 1],
            log_recv.at[step - 1],
            along_z(2 * step),
        )
        for step in range(1, 4)
    ]
    for copy in log_copies:
        copy.start()
    doc_row[...] = DOCS * doc_scale * live[...]

    def spread(at, _):
        line = jnp.broadcast_to(doc_row[pl.ds(at, 1), :], (BLOCK, BLOCK)).T
        doc_col[pl.ds(pl.multiple_of(at * BLOCK, BLOCK), BLOCK), :] = line
        return 0

    lax.fori_loop(0, BLOCKS, spread, 0)

    share = WIDTH // 8
    left_x, right_x, far_x = mod(x + 3, 4), mod(x + 1, 4), mod(x + 2, 4)
    to_up, to_down = along_x(1), along_x(3)

    def piece(owner, half):
        return pl.ds(pl.multiple_of(owner * (2 * share) + half * share, 8), share)

    halves = (pl.ds(0, share), pl.ds(share, share))

    def sum_copies(at):
        n, f, w = numer.at[at], far.at[at], near.at[at]
        plan = [
            (n.at[piece(far_x, 0)], f.at[0], to_down),
            (n.at[piece(far_x, 1)], f.at[1], to_up),
            (n.at[piece(left_x, 1)], w.at[1, halves[1]], to_down),
            (n.at[piece(right_x, 0)], w.at[0, halves[0]], to_up),
            (n.at[piece(left_x, 0)], w.at[1, halves[0]], to_down),
            (n.at[piece(right_x, 1)], w.at[0, halves[1]], to_up),
        ]
        return [
            remote(src, dst, sum_send.at[at * 6 + i], sum_recv.at[at * 6 + i], target)
            for i, (src, dst, target) in enumerate(plan)
        ]

    def quarter_of(at):
        return mod(hi + 1 + at, QUARTERS)

    def numerators(at):
        quarter = quarter_of(at)
        line = scale[quarter][None]

        def body(which, _):
            weights = score[quarter, pl.ds(pl.multiple_of(which * SLOTS, SLOTS), SLOTS), :]
            factor = wide(doc_col[pl.ds(pl.multiple_of(which * SLOTS, SLOTS), SLOTS), :])
            plan = (factor * weights).reshape(SLOTS // 8, 8, COLS) * line
            plan = plan.reshape(SLOTS, COLS).astype(BF16)
            term = jnp.dot(units_t[which], plan, preferred_element_type=F32)

            @pl.when(which == 0)
            def _():
                numer[at] = term

            @pl.when(which > 0)
            def _():
                numer[at] += term

            return 0

        lax.fori_loop(0, HOSTS, body, 0)

    def share_copy(at, half):
        target = quarter_of(at) * 2 + half
        return target, remote(
            reduced.at[at, halves[half]],
            shares.at[z],
            share_send.at[at * 2 + half],
            share_recv.at[z],
            device(x, y, target, core),
        )

    all_sums = [sum_copies(at) for at in range(QUARTERS)]

    def hand_on(at):
        copies = all_sums[at]
        copies[0].wait_recv()
        numer[at, piece(left_x, 0), :] += far[at, 0]
        copies[4].start()
        copies[1].wait_recv()
        numer[at, piece(right_x, 1), :] += far[at, 1]
        copies[5].start()

    def reduce_x(at):
        copies = all_sums[at]
        for i in (2, 3, 4, 5):
            copies[i].wait_recv()
        mine = numer[at, pl.ds(pl.multiple_of(x * (2 * share), 8), 2 * share), :]
        reduced[at] = mine + near[at, 0] + near[at, 1]
        for half in range(2):
            target, copy = share_copy(at, half)

            @pl.when(target != z)
            def _():
                copy.start()

            @pl.when(target == z)
            def _():
                shares[z] = reduced[at, halves[half], :]

    for at in range(QUARTERS):
        numerators(at)
        for i in range(4):
            all_sums[at][i].start()
        if at >= 1:
            hand_on(at - 1)
        if at >= 2:
            reduce_x(at - 2)

    for copy in log_copies:
        copy.wait()
    counts = jnp.concatenate(
        [doc_log[quarter, BLOCKS : BLOCKS + HOSTS, :] for quarter in range(QUARTERS)], axis=0
    )
    values = jnp.concatenate([doc_log[quarter, 0:BLOCKS, :] for quarter in range(QUARTERS)], axis=0)
    lane = lax.broadcasted_iota(jnp.int32, (32, BLOCK), 1)
    line = lax.broadcasted_iota(jnp.int32, (32, BLOCK), 0)
    owner = lane >> 2
    begin = jnp.sum(jnp.where(line < owner, counts, 0.0), axis=0, keepdims=True)
    held = jnp.sum(jnp.where(line == owner, counts, 0.0), axis=0, keepdims=True)
    slot = (lax.broadcasted_iota(jnp.int32, (1, BLOCK), 1) & 3).astype(F32)
    place = jnp.where(slot < held, begin + slot, -1.0)
    goal = jnp.full((1, BLOCK), -1.0, F32)
    for at in range(64):
        goal = jnp.where(place == float(at), dest_ref[0, at].astype(F32), goal)
    chosen = lax.broadcasted_iota(jnp.int32, (64, BLOCK), 0).astype(F32) == goal
    weights_out[...] = jnp.dot(
        jnp.where(chosen, 1.0, 0.0),
        values,
        precision=lax.Precision.HIGHEST,
        preferred_element_type=F32,
    )

    hand_on(3)
    reduce_x(2)
    reduce_x(3)
    for step in range(1, 8):
        other = mod(z + step, 8)
        remote(
            shares.at[other], shares.at[other], share_send.at[0], share_recv.at[other], along_z(1)
        ).wait_recv()
    total = shares[0]
    for other in range(1, 8):
        total = total + shares[other]
    numer_out[...] = total

    for at in range(QUARTERS):
        for copy in all_sums[at]:
            copy.wait_send()
        for half in range(2):
            target, copy = share_copy(at, half)

            @pl.when(target != z)
            def _():
                copy.wait_send()


def on_device(loader_blocks, block_counts, block_dest, centroids):
    dma = pltpu.SemaphoreType.DMA
    share = WIDTH // 8
    vmem = pl.BlockSpec(memory_space=pltpu.VMEM)
    smem = pl.BlockSpec(memory_space=pltpu.SMEM)
    numer, weights = pl.pallas_call(
        kernel,
        out_shape=(
            jax.ShapeDtypeStruct((share, COLS), F32),
            jax.ShapeDtypeStruct((64, BLOCK), F32),
        ),
        in_specs=[vmem, smem, smem, vmem],
        out_specs=(vmem, vmem),
        scratch_shapes=[
            pltpu.VMEM((HOSTS, SLOTS, WIDTH), BF16),
            pltpu.VMEM((HOSTS, WIDTH, SLOTS), BF16),
            pltpu.VMEM((QUARTERS, WIDTH, COLS), BF16),
            pltpu.VMEM((QUARTERS, HOSTS * SLOTS, COLS), F32),
            pltpu.VMEM((HOSTS, 8, BLOCK), F32),
            pltpu.VMEM((BLOCKS, BLOCK), F32),
            pltpu.VMEM((QUARTERS, 8, COLS), F32),
            pltpu.VMEM((2, 4, 8, 256), F32),
            pltpu.VMEM((2, 8, 8, 256), F32),
            pltpu.VMEM((QUARTERS, 8, COLS), F32),
            pltpu.VMEM((2, HOSTS, BLOCKS, BLOCK), F32),
            pltpu.VMEM((BLOCKS, BLOCK), F32),
            pltpu.VMEM((HOSTS * SLOTS, BLOCK), F32),
            pltpu.VMEM((QUARTERS, WIDTH, COLS), F32),
            pltpu.VMEM((QUARTERS, 2, share, COLS), F32),
            pltpu.VMEM((QUARTERS, 2, 2 * share, COLS), F32),
            pltpu.VMEM((QUARTERS, 2 * share, COLS), F32),
            pltpu.VMEM((8, share, COLS), F32),
            pltpu.VMEM((QUARTERS, BLOCKS + HOSTS, BLOCK), F32),
            dma((13,)),
            dma((13,)),
            dma((12,)),
            dma((12,)),
            dma((7,)),
            dma((7,)),
            dma((6,)),
            dma((6,)),
            dma((14,)),
            dma((14,)),
            dma((14,)),
            dma((14,)),
            dma((3,)),
            dma((3,)),
            dma((24,)),
            dma((24,)),
            dma((8,)),
            dma((8,)),
        ],
        compiler_params=pltpu.CompilerParams(
            collective_id=0, has_side_effects=True, vmem_limit_bytes=62 << 20
        ),
        cost_estimate=pl.CostEstimate(
            flops=13_000_000_000, bytes_accessed=2_000_000, transcendentals=8_400_000
        ),
    )(loader_blocks.reshape(SLOTS, WIDTH), block_counts, block_dest, centroids)
    return numer, weights.reshape(64 * BLOCK)


def solution(mesh):
    in_specs = (P("docs", "cent", None, None), P("docs", "cent"), P("docs", None), P(None, "cent"))
    out_specs = (P("docs", "cent"), P("docs"))
    return jax.shard_map(
        on_device, mesh=mesh, in_specs=in_specs, out_specs=out_specs, check_vma=False
    )
```

```python
import jax
import jax.numpy as jnp
from jax import lax
from jax.experimental import pallas as pl
from jax.experimental.pallas import tpu as pltpu
from jax.sharding import PartitionSpec as P

F32 = jnp.float32
BF16 = jnp.bfloat16

WIDTH = 384
COLS = 512
SLOTS = 512
BLOCK = 128
MOST = 4
HOSTS = 8
BLOCKS = HOSTS * MOST
QUARTERS = 4
SHARPNESS = 25.0
LOG2_E = 1.4426950408889634
STEP = 1.99
DOCS = 65536.0
CENTROIDS = 16384.0


def mod(value, size):
    return lax.rem(value, jnp.int32(size))


def wide(tile):
    return jnp.concatenate([tile] * (COLS // BLOCK), axis=1)


def device(x, y, z, core):
    return (x * 2 + mod(z, 2), (lax.div(z, jnp.int32(2)) * 4 + y) * 2 + core)


def kernel(
    docs_hbm,
    counts_ref,
    dest_ref,
    cents_hbm,
    numer_out,
    weights_out,
    units,
    units_t,
    cents,
    score,
    live_counts,
    live,
    col_acc,
    col_x,
    col_z,
    scale,
    rows,
    doc_row,
    doc_col,
    numer,
    out_x,
    in_x,
    out_z,
    in_z,
    reduced,
    doc_log,
    docs_ref,
    cents_ref,
    load_sem,
    unit_send,
    unit_recv,
    cent_send,
    cent_recv,
    count_send,
    count_recv,
    colx_send,
    colx_recv,
    colz_send,
    colz_recv,
    row_send,
    row_recv,
    log_send,
    log_recv,
    sum_send,
    sum_recv,
    share_send,
    share_recv,
):
    doc_index = lax.axis_index("docs")
    cent_index = lax.axis_index("cent")
    x = lax.div(doc_index, jnp.int32(2))
    lo = mod(doc_index, 2)
    core = mod(cent_index, 2)
    y = mod(lax.div(cent_index, jnp.int32(2)), 4)
    hi = lax.div(cent_index, jnp.int32(8))
    z = hi * 2 + lo
    host = y * 2 + core

    def along_host(step):
        other = mod(host + step, HOSTS)
        return device(x, lax.div(other, jnp.int32(2)), z, mod(other, 2))

    def along_x(step):
        return device(mod(x + step, 4), y, z, core)

    def along_z(step):
        return device(x, y, mod(z + step, 8), core)

    def along_y(step):
        return device(x, mod(y + step, 4), z, core)

    def remote(src, dst, send, recv, target):
        return pltpu.make_async_remote_copy(
            src_ref=src,
            dst_ref=dst,
            send_sem=send,
            recv_sem=recv,
            device_id=target,
            device_id_type=pl.DeviceIdType.MESH,
        )

    to_right, to_left = along_y(1), along_y(3)
    to_twin = device(x, y, z, 1 - core)

    barrier = pltpu.get_barrier_semaphore()
    greeted = [along_z(1), along_z(7)]
    greeted += [along_host(step) for step in range(1, 8)]
    greeted += [along_x(step) for step in range(1, 4)]
    for other in greeted:
        pl.semaphore_signal(
            barrier, inc=1, device_id=other, device_id_type=pl.DeviceIdType.MESH
        )
    load_docs = pltpu.make_async_copy(docs_hbm, docs_ref, load_sem.at[0])
    load_cents = pltpu.make_async_copy(cents_hbm, cents_ref, load_sem.at[1])
    load_docs.start()
    load_cents.start()

    load_docs.wait()
    values = docs_ref[...].astype(F32)
    factor = lax.rsqrt(jnp.mean(values * values, axis=1, keepdims=True) + 1e-06)
    units[host] = (values * factor * WIDTH ** (-0.5)).astype(BF16)
    load_cents.wait()
    values = cents_ref[...].astype(F32)
    factor = lax.rsqrt(jnp.mean(values * values, axis=0, keepdims=True) + 1e-06)
    cents[hi] = (values * factor * WIDTH ** (-0.5)).astype(BF16)
    live_counts[host] = jnp.full((8, BLOCK), counts_ref[0, 0].astype(F32), F32)
    col_acc[...] = jnp.zeros_like(col_acc)

    pl.semaphore_wait(barrier, 12)

    left_y, right_y, far_y = mod(y + 3, 4), mod(y + 1, 4), mod(y + 2, 4)
    first, second, whole = pl.ds(0, SLOTS // 2), pl.ds(SLOTS // 2, SLOTS // 2), pl.ds(0, SLOTS)
    own, from_left, from_right, across = (
        host,
        left_y * 2 + core,
        right_y * 2 + core,
        far_y * 2 + core,
    )
    unit_plan = [
        (own, first, to_right),
        (own, second, to_right),
        (own, first, to_left),
        (own, second, to_left),
        (from_left, first, to_right),
        (from_right, second, to_left),
        (own, whole, to_twin),
        (from_left, first, to_twin),
        (from_left, second, to_twin),
        (from_right, first, to_twin),
        (from_right, second, to_twin),
        (across, first, to_twin),
        (across, second, to_twin),
    ]
    unit_copies = []
    for at, (which, part, target) in enumerate(unit_plan):
        ref = units.at[which, part]
        unit_copies.append(remote(ref, ref, unit_send.at[at], unit_recv.at[at], target))

    chunk = WIDTH // 4
    rising, falling = [], []
    for step in range(6):
        back = 1 if step < 4 else 2
        which = mod(hi - back + lo + 4, QUARTERS)
        ref = cents.at[which, pl.ds((step % 4) * chunk, chunk)]
        rising.append(remote(ref, ref, cent_send.at[step], cent_recv.at[step], along_z(1)))
        ahead = 0 if step < 4 else 1
        which = mod(hi + ahead + lo, QUARTERS)
        ref = cents.at[which, pl.ds(((step + 2) % 4) * chunk, chunk)]
        falling.append(
            remote(ref, ref, cent_send.at[6 + step], cent_recv.at[6 + step], along_z(7))
        )

    def cent_open(steps):
        @pl.when(lo == 1)
        def _():
            for step in steps:
                rising[step].start()

        @pl.when(lo == 0)
        def _():
            for step in steps:
                falling[step].start()

    def cent_start(step):
        @pl.when(lo == 1)
        def _():
            if step >= 4:
                rising[step - 4].wait_recv()
                rising[step].start()
            falling[step].wait_recv()
            falling[step].start()

        @pl.when(lo == 0)
        def _():
            if step >= 4:
                falling[step - 4].wait_recv()
                falling[step].start()
            rising[step].wait_recv()
            rising[step].start()

    def cent_finish(steps):
        @pl.when(lo == 1)
        def _():
            for step in steps:
                rising[step].wait_recv()

        @pl.when(lo == 0)
        def _():
            for step in steps:
                falling[step].wait_recv()

    count_copies = [
        remote(
            live_counts.at[host],
            live_counts.at[host],
            count_send.at[step - 1],
            count_recv.at[step - 1],
            along_host(step),
        )
        for step in range(1, 8)
    ]
    def score_tiles(which, turns):
        for turn in turns:
            quarter = mod(hi + (turn ^ (turn >> 1)), QUARTERS)
            logits = jnp.dot(units[which], cents[quarter], preferred_element_type=F32)
            weights = jnp.exp2((SHARPNESS * LOG2_E) * logits)
            score[quarter, pl.ds(pl.multiple_of(which * SLOTS, SLOTS), SLOTS), :] = weights
            total = col_acc[quarter]
            for slot in range(MOST):
                part = weights[slot * BLOCK : (slot + 1) * BLOCK]
                part = jnp.sum(part.reshape(BLOCK // 8, 8, COLS), axis=0)
                here = jnp.where(live_counts[which] > slot, 1.0, 0.0)
                total = total + part * wide(here)
            col_acc[quarter] = total

    def score_hosts(count, host_of, turns, unroll):
        def body(at, _):
            score_tiles(host_of(at), turns)
            return 0

        lax.fori_loop(0, count, body, 0, unroll=unroll)

    def take(*numbers):
        for at in numbers:
            unit_copies[at].wait_recv()

    def give(*numbers):
        for at in numbers:
            unit_copies[at].start()

    give(0, 3)
    cent_open((0, 1))
    give(6)
    for copy in count_copies:
        copy.start()
    take(6)
    for copy in count_copies:
        copy.wait_recv()
    give(1, 2)
    cent_open((2, 3))
    score_hosts(2, lambda at: y * 2 + (core ^ at), (0,), 2)
    cent_start(0)
    take(0, 3)
    give(4, 5, 7, 10)
    cent_start(1)
    cent_start(2)
    take(1, 2)
    give(8, 9)
    cent_start(3)
    cent_start(4)
    take(7, 8, 9, 10)
    score_hosts(4, lambda at: mod(y + 1 + 2 * (at >> 1), 4) * 2 + (core ^ (at & 1)), (0,), 2)
    cent_start(5)
    cent_finish((2, 3))
    score_hosts(6, lambda at: mod(y + 3 + (at >> 1), 4) * 2 + (core ^ (at & 1)), (1, 2), 2)
    take(4, 5)
    give(11, 12)
    cent_finish((4, 5))
    score_hosts(6, lambda at: mod(y + 3 + (at >> 1), 4) * 2 + (core ^ (at & 1)), (3,), 3)
    take(11, 12)
    score_hosts(2, lambda at: far_y * 2 + (core ^ at), (0, 1, 2, 3), 2)

    for at in range(13):
        unit_copies[at].wait_send()
    for step in range(6):
        rising[step].wait_send()
        falling[step].wait_send()
    for copy in count_copies:
        copy.wait_send()

    for which in range(HOSTS):
        units_t[which] = units[which].T
        for slot in range(MOST):
            at = which * MOST + slot
            live[at : at + 1, :] = jnp.where(live_counts[which, 0:1, :] > slot, 1.0, 0.0)

    def exchange_columns(turn):
        for quarter in range(QUARTERS):
            total = jnp.sum(col_acc[quarter], axis=0, keepdims=True)
            for part in range(2):
                col_x[turn, x, 2 * quarter + part : 2 * quarter + part + 1, :] = total[
                    :, part * 256 : (part + 1) * 256
                ]
        copies = [
            remote(
                col_x.at[turn, x],
                col_x.at[turn, x],
                colx_send.at[turn * 3 + step - 1],
                colx_recv.at[turn * 3 + step - 1],
                along_x(step),
            )
            for step in range(1, 4)
        ]
        for copy in copies:
            copy.start()
        for copy in copies:
            copy.wait()
        col_z[turn, z] = (col_x[turn, 0] + col_x[turn, 1]) + (col_x[turn, 2] + col_x[turn, 3])
        copies = [
            remote(
                col_z.at[turn, z],
                col_z.at[turn, z],
                colz_send.at[turn * 7 + step - 1],
                colz_recv.at[turn * 7 + step - 1],
                along_z(step),
            )
            for step in range(1, 8)
        ]
        for copy in copies:
            copy.start()
        for copy in copies:
            copy.wait()
        total = col_z[turn, 0]
        for other in range(1, 8):
            total = total + col_z[turn, other]
        result = 1.0 / (CENTROIDS * total)
        for quarter in range(QUARTERS):
            line = jnp.concatenate(
                [result[2 * quarter : 2 * quarter + 1], result[2 * quarter + 1 : 2 * quarter + 2]],
                axis=1,
            )
            scale[quarter] = jnp.broadcast_to(line, (8, COLS))

    half_blocks = BLOCKS // 2

    def row_pass(turn, half):
        def body(at, _):
            total = None
            for quarter in range(QUARTERS):
                weights = score[quarter, pl.ds(pl.multiple_of(at * BLOCK, BLOCK), BLOCK), :]
                weights = weights.reshape(BLOCK // 8, 8, COLS) * scale[quarter][None]
                weights = weights.reshape(BLOCK, COLS)
                for part in range(COLS // BLOCK):
                    piece = weights[:, part * BLOCK : (part + 1) * BLOCK]
                    total = piece if total is None else total + piece
            rows[turn, host, pl.ds(at, 1), :] = jnp.sum(total.T, axis=0, keepdims=True)
            return 0

        lax.fori_loop(half * half_blocks, (half + 1) * half_blocks, body, 0, unroll=4)
        ref = rows.at[turn, host, pl.ds(half * half_blocks, half_blocks)]
        copies = []
        for step in range(1, 8):
            at = (turn * 2 + half) * 7 + step - 1
            copies.append(remote(ref, ref, row_send.at[at], row_recv.at[at], along_host(step)))
        for copy in copies:
            copy.start()
        return copies

    def doc_scales(turn, half, copies):
        for copy in copies:
            copy.wait()
        part = slice(half * half_blocks, (half + 1) * half_blocks)
        total = rows[turn, 0, part, :]
        for other in range(1, HOSTS):
            total = total + rows[turn, other, part, :]
        return part, 1.0 / (DOCS * total)

    exchange_columns(0)

    col_acc[...] = jnp.zeros_like(col_acc)

    def column_body(at, _):
        line = wide(jnp.broadcast_to(doc_row[pl.ds(at, 1), :], (BLOCK, BLOCK)).T)
        for quarter in range(QUARTERS):
            weights = score[quarter, pl.ds(pl.multiple_of(at * BLOCK, BLOCK), BLOCK), :] * line
            col_acc[quarter] += jnp.sum(weights.reshape(BLOCK // 8, 8, COLS), axis=0)
        return 0

    sent = [row_pass(0, half) for half in range(2)]
    for half in range(2):
        part, doc_scale = doc_scales(0, half, sent[half])
        doc_row[part, :] = doc_scale * live[part, :]
        lax.fori_loop(half * half_blocks, (half + 1) * half_blocks, column_body, 0, unroll=4)
    exchange_columns(1)

    def spread(at, _):
        line = jnp.broadcast_to(doc_row[pl.ds(at, 1), :], (BLOCK, BLOCK)).T
        doc_col[pl.ds(pl.multiple_of(at * BLOCK, BLOCK), BLOCK), :] = line
        return 0

    share = WIDTH // 8
    tall = 2 * share

    def encode(values, ref):
        most = jnp.max(jnp.abs(values), axis=0, keepdims=True)
        power = jnp.ceil(jnp.log2(jnp.maximum(most, 1e-30)))
        steps = jnp.round(values * (jnp.exp2(14.0 - power) * STEP))
        count = values.shape[0]
        ref[0:count, :] = steps.astype(jnp.int32).astype(jnp.int16)
        ref[count : count + 16, :] = (
            jnp.broadcast_to(power, (16, COLS)).astype(jnp.int32).astype(jnp.int16)
        )

    def decode(ref, count):
        power = ref[count : count + 16, :].astype(jnp.int32).astype(F32)[0:1]
        steps = ref[0:count, :].astype(jnp.int32).astype(F32)
        return steps * (jnp.exp2(power - 14.0) * (1.0 / STEP))

    def rows_of(owner):
        return pl.ds(pl.multiple_of(owner * tall, 8), tall)

    def sum_copies(at):
        return [
            remote(
                out_x.at[at, step - 1],
                in_x.at[at, step - 1],
                sum_send.at[at * 3 + step - 1],
                sum_recv.at[at * 3 + step - 1],
                along_x(step),
            )
            for step in range(1, 4)
        ]

    def quarter_of(at):
        return mod(hi + 1 + at, QUARTERS)

    def numerators(at, half):
        quarter = quarter_of(at)
        line = scale[quarter][None]
        total = None
        for which in range(half * HOSTS // 2, (half + 1) * HOSTS // 2):
            here = slice(which * SLOTS, (which + 1) * SLOTS)
            factor = wide(doc_col[here, :])
            plan = (factor * score[quarter, here, :]).reshape(SLOTS // 8, 8, COLS) * line
            plan = plan.reshape(SLOTS, COLS).astype(BF16)
            term = jnp.dot(units_t[which], plan, preferred_element_type=F32)
            total = term if total is None else total + term
        if half == 0:
            numer[at] = total
        else:
            numer[at] += total

    def share_copy(at, half):
        return remote(
            out_z.at[at, half],
            in_z.at[z],
            share_send.at[at * 2 + half],
            share_recv.at[z],
            device(x, y, quarter_of(at) * 2 + half, core),
        )

    last = QUARTERS - 1
    other_half = pl.ds(pl.multiple_of((1 - lo) * share, 8), share)
    own_half = pl.ds(pl.multiple_of(lo * share, 8), share)
    all_sums = [sum_copies(at) for at in range(QUARTERS)]
    all_shares = [share_copy(at, half) for at in range(last) for half in range(2)]
    all_shares.append(
        remote(
            out_z.at[last, 0],
            in_z.at[z],
            share_send.at[last * 2],
            share_recv.at[z],
            device(x, y, hi * 2 + 1 - lo, core),
        )
    )

    def send_x(at):
        for step in (2, 1, 3):
            encode(numer[at, rows_of(mod(x + step, 4)), :], out_x.at[at, step - 1])
            all_sums[at][step - 1].start()

    def reduce_x(at):
        total = numer[at, rows_of(x), :]
        for step in (1, 3, 2):
            all_sums[at][step - 1].wait_recv()
            total = total + decode(in_x.at[at, step - 1], tall)
        if at < last:
            for half in range(2):
                encode(total[half * share : (half + 1) * share], out_z.at[at, half])
                all_shares[at * 2 + half].start()
        else:
            reduced[...] = total
            encode(reduced[other_half, :], out_z.at[last, 0])
            all_shares[-1].start()

    sent = [row_pass(1, half) for half in range(2)]
    for half in range(2):
        part, doc_scale = doc_scales(1, half, sent[half])
        doc_log[hi, part, :] = jnp.log(DOCS * doc_scale)
        doc_row[part, :] = DOCS * doc_scale * live[part, :]
        lax.fori_loop(half * half_blocks, (half + 1) * half_blocks, spread, 0, unroll=4)
        numerators(0, half)
    for which in range(HOSTS):
        doc_log[hi, BLOCKS + which : BLOCKS + which + 1, :] = live_counts[which, 0:1, :]
    log_copies = [
        remote(
            doc_log.at[hi],
            doc_log.at[hi],
            log_send.at[step - 1],
            log_recv.at[step - 1],
            along_z(2 * step),
        )
        for step in range(1, 4)
    ]
    for copy in log_copies:
        copy.start()

    for at in range(QUARTERS):
        if at > 0:
            numerators(at, 0)
            numerators(at, 1)
        send_x(at)
        if at >= 2:
            reduce_x(at - 2)

    for copy in log_copies:
        copy.wait()
    counts = jnp.concatenate(
        [doc_log[quarter, BLOCKS : BLOCKS + HOSTS, :] for quarter in range(QUARTERS)], axis=0
    )
    values = jnp.concatenate([doc_log[quarter, 0:BLOCKS, :] for quarter in range(QUARTERS)], axis=0)
    lane = lax.broadcasted_iota(jnp.int32, (32, BLOCK), 1)
    line = lax.broadcasted_iota(jnp.int32, (32, BLOCK), 0)
    owner = lane >> 2
    begin = jnp.sum(jnp.where(line < owner, counts, 0.0), axis=0, keepdims=True)
    held = jnp.sum(jnp.where(line == owner, counts, 0.0), axis=0, keepdims=True)
    slot = (lax.broadcasted_iota(jnp.int32, (1, BLOCK), 1) & 3).astype(F32)
    place = jnp.where(slot < held, begin + slot, -1.0)
    goal = jnp.full((1, BLOCK), -1.0, F32)
    for at in range(64):
        goal = jnp.where(place == float(at), dest_ref[0, at].astype(F32), goal)
    chosen = lax.broadcasted_iota(jnp.int32, (64, BLOCK), 0).astype(F32) == goal
    weights_out[...] = jnp.dot(
        jnp.where(chosen, 1.0, 0.0),
        values,
        precision=lax.Precision.HIGHEST,
        preferred_element_type=F32,
    )

    reduce_x(2)
    reduce_x(3)
    total = reduced[own_half, :]
    for step in range(1, 8):
        other = mod(z + step, 8)
        remote(
            in_z.at[other], in_z.at[other], share_send.at[0], share_recv.at[other], along_z(1)
        ).wait_recv()
        total = total + decode(in_z.at[other], share)
    numer_out[...] = total

    for at in range(QUARTERS):
        for copy in all_sums[at]:
            copy.wait_send()
    for copy in all_shares:
        copy.wait_send()


def on_device(loader_blocks, block_counts, block_dest, centroids):
    dma = pltpu.SemaphoreType.DMA
    share = WIDTH // 8
    vmem = pl.BlockSpec(memory_space=pltpu.VMEM)
    smem = pl.BlockSpec(memory_space=pltpu.SMEM)
    anywhere = pl.BlockSpec(memory_space=pl.ANY)
    numer, weights = pl.pallas_call(
        kernel,
        out_shape=(
            jax.ShapeDtypeStruct((share, COLS), F32),
            jax.ShapeDtypeStruct((64, BLOCK), F32),
        ),
        in_specs=[anywhere, smem, smem, anywhere],
        out_specs=(vmem, vmem),
        scratch_shapes=[
            pltpu.VMEM((HOSTS, SLOTS, WIDTH), BF16),
            pltpu.VMEM((HOSTS, WIDTH, SLOTS), BF16),
            pltpu.VMEM((QUARTERS, WIDTH, COLS), BF16),
            pltpu.VMEM((QUARTERS, HOSTS * SLOTS, COLS), F32),
            pltpu.VMEM((HOSTS, 8, BLOCK), F32),
            pltpu.VMEM((BLOCKS, BLOCK), F32),
            pltpu.VMEM((QUARTERS, 8, COLS), F32),
            pltpu.VMEM((2, 4, 8, 256), F32),
            pltpu.VMEM((2, 8, 8, 256), F32),
            pltpu.VMEM((QUARTERS, 8, COLS), F32),
            pltpu.VMEM((2, HOSTS, BLOCKS, BLOCK), F32),
            pltpu.VMEM((BLOCKS, BLOCK), F32),
            pltpu.VMEM((HOSTS * SLOTS, BLOCK), F32),
            pltpu.VMEM((QUARTERS, WIDTH, COLS), F32),
            pltpu.VMEM((QUARTERS, 3, 2 * share + 16, COLS), jnp.int16),
            pltpu.VMEM((QUARTERS, 3, 2 * share + 16, COLS), jnp.int16),
            pltpu.VMEM((QUARTERS, 2, share + 16, COLS), jnp.int16),
            pltpu.VMEM((8, share + 16, COLS), jnp.int16),
            pltpu.VMEM((2 * share, COLS), F32),
            pltpu.VMEM((QUARTERS, BLOCKS + HOSTS, BLOCK), F32),
            pltpu.VMEM((SLOTS, WIDTH), BF16),
            pltpu.VMEM((WIDTH, COLS), BF16),
            dma((2,)),
            dma((13,)),
            dma((13,)),
            dma((12,)),
            dma((12,)),
            dma((7,)),
            dma((7,)),
            dma((6,)),
            dma((6,)),
            dma((14,)),
            dma((14,)),
            dma((28,)),
            dma((28,)),
            dma((3,)),
            dma((3,)),
            dma((12,)),
            dma((12,)),
            dma((8,)),
            dma((8,)),
        ],
        compiler_params=pltpu.CompilerParams(
            collective_id=0, has_side_effects=True, vmem_limit_bytes=62 << 20
        ),
        cost_estimate=pl.CostEstimate(
            flops=13_000_000_000, bytes_accessed=2_000_000, transcendentals=8_400_000
        ),
    )(loader_blocks.reshape(SLOTS, WIDTH), block_counts, block_dest, centroids)
    return numer, weights.reshape(64 * BLOCK)


def solution(mesh):
    in_specs = (P("docs", "cent", None, None), P("docs", "cent"), P("docs", None), P(None, "cent"))
    out_specs = (P("docs", "cent"), P("docs"))
    return jax.shard_map(
        on_device, mesh=mesh, in_specs=in_specs, out_specs=out_specs, check_vma=False
    )
```

```python
import jax
import jax.numpy as jnp
from jax import lax
from jax.experimental import pallas as pl
from jax.experimental.pallas import tpu as pltpu
from jax.sharding import PartitionSpec as P

F32 = jnp.float32
BF16 = jnp.bfloat16

WIDTH = 384
COLS = 512
SLOTS = 512
BLOCK = 128
MOST = 4
HOSTS = 8
BLOCKS = HOSTS * MOST
QUARTERS = 4
SHARPNESS = 25.0
LOG2_E = 1.4426950408889634
STEP = 1.99
DOCS = 65536.0
CENTROIDS = 16384.0


def mod(value, size):
    return lax.rem(value, jnp.int32(size))


def wide(tile):
    return jnp.concatenate([tile] * (COLS // BLOCK), axis=1)


def device(x, y, z, core):
    return (x * 2 + mod(z, 2), (lax.div(z, jnp.int32(2)) * 4 + y) * 2 + core)


def kernel(
    docs_hbm,
    counts_ref,
    dest_ref,
    cents_hbm,
    numer_out,
    weights_out,
    units,
    cents,
    score,
    live_counts,
    live,
    col_acc,
    col_x,
    col_z,
    scale,
    rows,
    doc_row,
    doc_col,
    numer,
    open_out,
    open_in,
    close_out,
    close_in,
    out_z,
    in_z,
    reduced,
    doc_log,
    docs_ref,
    cents_ref,
    load_sem,
    unit_send,
    unit_recv,
    cent_send,
    cent_recv,
    count_send,
    count_recv,
    colx_send,
    colx_recv,
    colz_send,
    colz_recv,
    row_send,
    row_recv,
    log_send,
    log_recv,
    sum_send,
    sum_recv,
    share_send,
    share_recv,
):
    doc_index = lax.axis_index("docs")
    cent_index = lax.axis_index("cent")
    x = lax.div(doc_index, jnp.int32(2))
    lo = mod(doc_index, 2)
    core = mod(cent_index, 2)
    y = mod(lax.div(cent_index, jnp.int32(2)), 4)
    hi = lax.div(cent_index, jnp.int32(8))
    z = hi * 2 + lo
    host = y * 2 + core

    def along_host(step):
        other = mod(host + step, HOSTS)
        return device(x, lax.div(other, jnp.int32(2)), z, mod(other, 2))

    def along_x(step):
        return device(mod(x + step, 4), y, z, core)

    def along_z(step):
        return device(x, y, mod(z + step, 8), core)

    def along_y(step):
        return device(x, mod(y + step, 4), z, core)

    def remote(src, dst, send, recv, target):
        return pltpu.make_async_remote_copy(
            src_ref=src,
            dst_ref=dst,
            send_sem=send,
            recv_sem=recv,
            device_id=target,
            device_id_type=pl.DeviceIdType.MESH,
        )

    to_right, to_left = along_y(1), along_y(3)
    to_twin = device(x, y, z, 1 - core)

    barrier = pltpu.get_barrier_semaphore()
    greeted = [along_z(1), along_z(7)]
    greeted += [along_host(step) for step in range(1, 8)]
    greeted += [along_x(step) for step in range(1, 4)]
    for other in greeted:
        pl.semaphore_signal(
            barrier, inc=1, device_id=other, device_id_type=pl.DeviceIdType.MESH
        )
    load_docs = pltpu.make_async_copy(docs_hbm, docs_ref, load_sem.at[0])
    load_cents = pltpu.make_async_copy(cents_hbm, cents_ref, load_sem.at[1])
    load_docs.start()
    load_cents.start()

    load_docs.wait()
    values = docs_ref[...].astype(F32)
    factor = lax.rsqrt(jnp.mean(values * values, axis=1, keepdims=True) + 1e-06)
    units[host] = (values * factor * WIDTH ** (-0.5)).astype(BF16)
    load_cents.wait()
    values = cents_ref[...].astype(F32)
    factor = lax.rsqrt(jnp.mean(values * values, axis=0, keepdims=True) + 1e-06)
    cents[hi] = (values * factor * WIDTH ** (-0.5)).astype(BF16)
    live_counts[host] = jnp.full((8, BLOCK), counts_ref[0, 0].astype(F32), F32)
    col_acc[...] = jnp.zeros_like(col_acc)

    def score_tiles(which, quarters):
        for quarter in quarters:
            logits = jnp.dot(units[which], cents[quarter], preferred_element_type=F32)
            weights = jnp.exp2((SHARPNESS * LOG2_E) * logits)
            score[quarter, pl.ds(pl.multiple_of(which * SLOTS, SLOTS), SLOTS), :] = weights
            total = col_acc[quarter]
            for slot in range(MOST):
                part = weights[slot * BLOCK : (slot + 1) * BLOCK]
                part = jnp.sum(part.reshape(BLOCK // 8, 8, COLS), axis=0)
                here = jnp.where(live_counts[which] > slot, 1.0, 0.0)
                total = total + part * wide(here)
            col_acc[quarter] = total

    left_y, right_y, far_y = mod(y + 3, 4), mod(y + 1, 4), mod(y + 2, 4)
    first, second, whole = pl.ds(0, SLOTS // 2), pl.ds(SLOTS // 2, SLOTS // 2), pl.ds(0, SLOTS)
    own, from_left, from_right, across = (
        host,
        left_y * 2 + core,
        right_y * 2 + core,
        far_y * 2 + core,
    )
    unit_plan = [
        (own, first, to_right),
        (own, second, to_right),
        (own, first, to_left),
        (own, second, to_left),
        (from_left, first, to_right),
        (from_right, second, to_left),
        (own, whole, to_twin),
        (from_left, first, to_twin),
        (from_left, second, to_twin),
        (from_right, first, to_twin),
        (from_right, second, to_twin),
        (across, first, to_twin),
        (across, second, to_twin),
    ]
    unit_copies = []
    for at, (which, part, target) in enumerate(unit_plan):
        ref = units.at[which, part]
        unit_copies.append(remote(ref, ref, unit_send.at[at], unit_recv.at[at], target))

    chunk = WIDTH // 8
    relay_way, origin_way = lo, 1 - lo
    relay_to, origin_to = along_z(1 + 6 * lo), along_z(7 - 6 * lo)
    relay_quarter = mod(hi + 3 + 2 * lo, QUARTERS)
    other_quarter = mod(hi + 5 - 2 * lo, QUARTERS)
    far_quarter = mod(hi + 2, QUARTERS)
    relays, origins = [], []
    for step in range(12):
        for copies, way, target, blocks in (
            (relays, relay_way, relay_to, (relay_quarter, far_quarter)),
            (origins, origin_way, origin_to, (hi, other_quarter)),
        ):
            line = mod(step + 4 * way, 8) * chunk
            ref = cents.at[blocks[step // 8], pl.ds(pl.multiple_of(line, 16), chunk)]
            at = way * 12 + step
            copies.append(remote(ref, ref, cent_send.at[at], cent_recv.at[at], target))

    count_copies = [
        remote(
            live_counts.at[host],
            live_counts.at[host],
            count_send.at[step - 1],
            count_recv.at[step - 1],
            along_host(step),
        )
        for step in range(1, 8)
    ]

    def take(*numbers):
        for at in numbers:
            unit_copies[at].wait_recv()

    def give(*numbers):
        for at in numbers:
            unit_copies[at].start()

    def relay(*steps):
        for step in steps:
            relays[step].wait_recv()
            relays[step].start()

    def onward(*steps):
        for step in steps:
            origins[step].wait_recv()
            origins[step + 8].start()

    def score_hosts(count, host_of, quarters, unroll):
        def body(at, _):
            score_tiles(host_of(at), quarters)
            return 0

        lax.fori_loop(0, count, body, 0, unroll=unroll)

    def here(at):
        return y * 2 + (core ^ at)

    def sides(at):
        return mod(y + 1 + 2 * at, 4) * 2 + core

    def sides_twin(at):
        return mod(y + 1 + 2 * at, 4) * 2 + 1 - core

    def near(at):
        return mod(y + 3 + (at >> 1), 4) * 2 + (core ^ (at & 1))

    score_tiles(host, (hi,))
    pl.semaphore_wait(barrier, 12)

    for copy in count_copies:
        copy.start()
    give(0, 3, 6)
    for step in range(8):
        origins[step].start()
    give(1, 2)
    relay(0)
    for copy in count_copies:
        copy.wait_recv()
    take(6)
    score_tiles(host ^ 1, (hi,))
    relay(1, 2, 3)
    take(0, 3)
    give(4, 5, 7, 10)
    relay(4, 5)
    onward(0)
    relay(6)
    onward(1)
    relay(7)
    onward(2)
    take(1, 2)
    give(8, 9)
    onward(3)
    score_hosts(2, here, (relay_quarter,), 2)
    relay(8)
    score_hosts(2, sides, (hi, relay_quarter), 2)
    relay(9)
    take(7, 8, 9, 10)
    relay(10)
    score_hosts(2, sides_twin, (hi, relay_quarter), 2)
    relay(11)
    take(4, 5)
    give(11, 12)
    for step in range(4, 8):
        origins[step].wait_recv()
    score_hosts(6, near, (other_quarter,), 3)
    score_tiles(across, (hi, relay_quarter, other_quarter))
    for step in range(8, 12):
        origins[step].wait_recv()
    score_hosts(6, near, (far_quarter,), 3)
    take(11, 12)
    score_tiles(across, (far_quarter,))
    score_tiles(across ^ 1, (hi, relay_quarter, other_quarter, far_quarter))

    for at in range(13):
        unit_copies[at].wait_send()
    for step in range(12):
        relays[step].wait_send()
        origins[step].wait_send()
    for copy in count_copies:
        copy.wait_send()

    for which in range(HOSTS):
        for slot in range(MOST):
            at = which * MOST + slot
            live[at : at + 1, :] = jnp.where(live_counts[which, 0:1, :] > slot, 1.0, 0.0)

    def exchange_columns(turn):
        for quarter in range(QUARTERS):
            total = jnp.sum(col_acc[quarter], axis=0, keepdims=True)
            for part in range(2):
                col_x[turn, x, 2 * quarter + part : 2 * quarter + part + 1, :] = total[
                    :, part * 256 : (part + 1) * 256
                ]
        copies = [
            remote(
                col_x.at[turn, x],
                col_x.at[turn, x],
                colx_send.at[turn * 3 + step - 1],
                colx_recv.at[turn * 3 + step - 1],
                along_x(step),
            )
            for step in range(1, 4)
        ]
        for copy in copies:
            copy.start()
        for copy in copies:
            copy.wait()
        col_z[turn, z] = (col_x[turn, 0] + col_x[turn, 1]) + (col_x[turn, 2] + col_x[turn, 3])
        copies = [
            remote(
                col_z.at[turn, z],
                col_z.at[turn, z],
                colz_send.at[turn * 7 + step - 1],
                colz_recv.at[turn * 7 + step - 1],
                along_z(step),
            )
            for step in range(1, 8)
        ]
        for copy in copies:
            copy.start()
        for copy in copies:
            copy.wait()
        total = col_z[turn, 0]
        for other in range(1, 8):
            total = total + col_z[turn, other]
        result = 1.0 / (CENTROIDS * total)
        for quarter in range(QUARTERS):
            line = jnp.concatenate(
                [result[2 * quarter : 2 * quarter + 1], result[2 * quarter + 1 : 2 * quarter + 2]],
                axis=1,
            )
            scale[quarter] = jnp.broadcast_to(line, (8, COLS))

    half_blocks = BLOCKS // 2

    def row_pass(turn, half):
        def body(at, _):
            total = None
            for quarter in range(QUARTERS):
                weights = score[quarter, pl.ds(pl.multiple_of(at * BLOCK, BLOCK), BLOCK), :]
                weights = weights.reshape(BLOCK // 8, 8, COLS) * scale[quarter][None]
                weights = weights.reshape(BLOCK, COLS)
                for part in range(COLS // BLOCK):
                    piece = weights[:, part * BLOCK : (part + 1) * BLOCK]
                    total = piece if total is None else total + piece
            rows[turn, host, pl.ds(at, 1), :] = jnp.sum(total.T, axis=0, keepdims=True)
            return 0

        lax.fori_loop(half * half_blocks, (half + 1) * half_blocks, body, 0, unroll=4)
        ref = rows.at[turn, host, pl.ds(half * half_blocks, half_blocks)]
        copies = []
        for step in range(1, 8):
            at = (turn * 2 + half) * 7 + step - 1
            copies.append(remote(ref, ref, row_send.at[at], row_recv.at[at], along_host(step)))
        for copy in copies:
            copy.start()
        return copies

    def doc_scales(turn, half, copies):
        for copy in copies:
            copy.wait()
        part = slice(half * half_blocks, (half + 1) * half_blocks)
        total = rows[turn, 0, part, :]
        for other in range(1, HOSTS):
            total = total + rows[turn, other, part, :]
        return part, 1.0 / (DOCS * total)

    exchange_columns(0)

    col_acc[...] = jnp.zeros_like(col_acc)

    def column_body(at, _):
        line = wide(jnp.broadcast_to(doc_row[pl.ds(at, 1), :], (BLOCK, BLOCK)).T)
        for quarter in range(QUARTERS):
            weights = score[quarter, pl.ds(pl.multiple_of(at * BLOCK, BLOCK), BLOCK), :] * line
            col_acc[quarter] += jnp.sum(weights.reshape(BLOCK // 8, 8, COLS), axis=0)
        return 0

    sent = [row_pass(0, half) for half in range(2)]
    for half in range(2):
        part, doc_scale = doc_scales(0, half, sent[half])
        doc_row[part, :] = doc_scale * live[part, :]
        lax.fori_loop(half * half_blocks, (half + 1) * half_blocks, column_body, 0, unroll=4)
    exchange_columns(1)

    def spread(at, _):
        line = jnp.broadcast_to(doc_row[pl.ds(at, 1), :], (BLOCK, BLOCK)).T
        doc_col[pl.ds(pl.multiple_of(at * BLOCK, BLOCK), BLOCK), :] = line
        return 0

    share = WIDTH // 8
    tall = 2 * share
    groups = COLS // BLOCK

    def encode(pieces, ref):
        row = lax.broadcasted_iota(jnp.int32, (16, BLOCK), 0)
        powers = jnp.zeros((16, BLOCK), F32)
        for at, values in enumerate(pieces):
            most = jnp.max(jnp.abs(values), axis=0, keepdims=True)
            power = jnp.ceil(jnp.log2(jnp.maximum(most, 1e-30)))
            steps = jnp.round(values * (jnp.exp2(14.0 - power) * STEP))
            steps = steps.astype(jnp.int32).astype(jnp.int16)
            for group in range(groups):
                place = at * groups + group
                lanes = slice(group * BLOCK, (group + 1) * BLOCK)
                ref[place * share : (place + 1) * share, :] = steps[:, lanes]
                powers = jnp.where(row == place, power[:, lanes], powers)
        end = len(pieces) * groups * share
        ref[end : end + 16, :] = powers.astype(jnp.int32).astype(jnp.int16)

    def decode(ref, at, count):
        end = count * groups * share
        powers = ref[end : end + 16, :].astype(jnp.int32).astype(F32)
        factors = jnp.exp2(powers - 14.0) * (1.0 / STEP)
        out = []
        for group in range(groups):
            place = at * groups + group
            steps = ref[place * share : (place + 1) * share, :].astype(jnp.int32).astype(F32)
            out.append(steps * factors[place : place + 1])
        return jnp.concatenate(out, axis=1)

    left_x, right_x, far_x = mod(x + 3, 4), mod(x + 1, 4), mod(x + 2, 4)

    def piece(at, owner, half):
        return numer[at, pl.ds(pl.multiple_of(owner * tall + half * share, 8), share), :]

    ways = ((1, right_x, 1), (3, left_x, 0))

    def sum_copies(at):
        opening, closing = [], []
        for way, (step, _, _) in enumerate(ways):
            place = at * 4 + way * 2
            opening.append(
                remote(
                    open_out.at[at, way],
                    open_in.at[at, way],
                    sum_send.at[place],
                    sum_recv.at[place],
                    along_x(step),
                )
            )
            closing.append(
                remote(
                    close_out.at[at, way],
                    close_in.at[at, way],
                    sum_send.at[place + 1],
                    sum_recv.at[place + 1],
                    along_x(step),
                )
            )
        return opening, closing

    def quarter_of(at):
        return mod(hi + (2, 1, 3, 0)[at], QUARTERS)

    def numerators(at, half):
        quarter = quarter_of(at)
        line = scale[quarter][None]
        total = None
        for which in range(half * HOSTS // 2, (half + 1) * HOSTS // 2):
            here = slice(which * SLOTS, (which + 1) * SLOTS)
            factor = wide(doc_col[here, :])
            plan = (factor * score[quarter, here, :]).reshape(SLOTS // 8, 8, COLS) * line
            plan = plan.reshape(SLOTS, COLS).astype(BF16)
            term = lax.dot_general(
                units[which], plan, (((0,), (0,)), ((), ())), preferred_element_type=F32
            )
            total = term if total is None else total + term
        if half == 0:
            numer[at] = total
        else:
            numer[at] += total

    def share_copy(at, half):
        return remote(
            out_z.at[at, half],
            in_z.at[z],
            share_send.at[at * 2 + half],
            share_recv.at[z],
            device(x, y, quarter_of(at) * 2 + half, core),
        )

    last = QUARTERS - 1
    other_half = pl.ds(pl.multiple_of((1 - lo) * share, 8), share)
    own_half = pl.ds(pl.multiple_of(lo * share, 8), share)
    all_sums = [sum_copies(at) for at in range(QUARTERS)]
    all_shares = [share_copy(at, half) for at in range(last) for half in range(2)]
    all_shares.append(
        remote(
            out_z.at[last, 0],
            in_z.at[z],
            share_send.at[last * 2],
            share_recv.at[z],
            device(x, y, hi * 2 + 1 - lo, core),
        )
    )

    def open_x(at):
        for way, (_, owner, half) in enumerate(ways):
            encode([piece(at, far_x, half), piece(at, owner, 1 - half)], open_out.at[at, way])
            all_sums[at][0][way].start()

    def close_x(at):
        for way, (_, owner, half) in enumerate(ways):
            all_sums[at][0][way].wait_recv()
            total = piece(at, owner, half) + decode(open_in.at[at, way], 0, 2)
            encode([total], close_out.at[at, way])
            all_sums[at][1][way].start()

    def reduce_x(at):
        for way, (_, _, half) in enumerate(ways):
            all_sums[at][1][way].wait_recv()
            total = piece(at, x, half) + decode(open_in.at[at, 1 - way], 1, 2)
            total = total + decode(close_in.at[at, way], 0, 1)
            if at < last:
                encode([total], out_z.at[at, half])
                all_shares[at * 2 + half].start()
            else:
                reduced[half * share : (half + 1) * share, :] = total
        if at == last:
            encode([reduced[other_half, :]], out_z.at[last, 0])
            all_shares[-1].start()

    sent = [row_pass(1, half) for half in range(2)]
    for half in range(2):
        part, doc_scale = doc_scales(1, half, sent[half])
        doc_log[hi, part, :] = jnp.log(DOCS * doc_scale)
        doc_row[part, :] = DOCS * doc_scale * live[part, :]
        lax.fori_loop(half * half_blocks, (half + 1) * half_blocks, spread, 0, unroll=4)
        numerators(0, half)
    for which in range(HOSTS):
        doc_log[hi, BLOCKS + which : BLOCKS + which + 1, :] = live_counts[which, 0:1, :]
    log_copies = [
        remote(
            doc_log.at[hi],
            doc_log.at[hi],
            log_send.at[step - 1],
            log_recv.at[step - 1],
            along_z(2 * step),
        )
        for step in range(1, 4)
    ]
    for copy in log_copies:
        copy.start()

    for at in range(QUARTERS):
        if at > 0:
            numerators(at, 0)
            numerators(at, 1)
        if at >= 2:
            close_x(at - 2)
        open_x(at)
    close_x(2)
    reduce_x(0)
    reduce_x(1)

    for copy in log_copies:
        copy.wait()
    counts = jnp.concatenate(
        [doc_log[quarter, BLOCKS : BLOCKS + HOSTS, :] for quarter in range(QUARTERS)], axis=0
    )
    values = jnp.concatenate([doc_log[quarter, 0:BLOCKS, :] for quarter in range(QUARTERS)], axis=0)
    lane = lax.broadcasted_iota(jnp.int32, (32, BLOCK), 1)
    line = lax.broadcasted_iota(jnp.int32, (32, BLOCK), 0)
    owner = lane >> 2
    begin = jnp.sum(jnp.where(line < owner, counts, 0.0), axis=0, keepdims=True)
    held = jnp.sum(jnp.where(line == owner, counts, 0.0), axis=0, keepdims=True)
    slot = (lax.broadcasted_iota(jnp.int32, (1, BLOCK), 1) & 3).astype(F32)
    place = jnp.where(slot < held, begin + slot, -1.0)
    goal = jnp.full((1, BLOCK), -1.0, F32)
    for at in range(64):
        goal = jnp.where(place == float(at), dest_ref[0, at].astype(F32), goal)
    chosen = lax.broadcasted_iota(jnp.int32, (64, BLOCK), 0).astype(F32) == goal
    weights_out[...] = jnp.dot(
        jnp.where(chosen, 1.0, 0.0),
        values,
        precision=lax.Precision.HIGHEST,
        preferred_element_type=F32,
    )

    close_x(3)
    reduce_x(2)
    reduce_x(3)
    total = reduced[own_half, :]
    for step in range(1, 8):
        other = mod(z + step, 8)
        remote(
            in_z.at[other], in_z.at[other], share_send.at[0], share_recv.at[other], along_z(1)
        ).wait_recv()
        total = total + decode(in_z.at[other], 0, 1)
    numer_out[...] = total

    for at in range(QUARTERS):
        for copy in all_sums[at][0] + all_sums[at][1]:
            copy.wait_send()
    for copy in all_shares:
        copy.wait_send()


def on_device(loader_blocks, block_counts, block_dest, centroids):
    dma = pltpu.SemaphoreType.DMA
    share = WIDTH // 8
    single = share * (COLS // BLOCK) + 16
    double = 2 * share * (COLS // BLOCK) + 16
    vmem = pl.BlockSpec(memory_space=pltpu.VMEM)
    smem = pl.BlockSpec(memory_space=pltpu.SMEM)
    anywhere = pl.BlockSpec(memory_space=pl.ANY)
    numer, weights = pl.pallas_call(
        kernel,
        out_shape=(
            pltpu.VMEM((share, COLS), F32),
            pltpu.VMEM((64, BLOCK), F32),
        ),
        in_specs=[anywhere, smem, smem, anywhere],
        out_specs=(vmem, vmem),
        scratch_shapes=[
            pltpu.VMEM((HOSTS, SLOTS, WIDTH), BF16),
            pltpu.VMEM((QUARTERS, WIDTH, COLS), BF16),
            pltpu.VMEM((QUARTERS, HOSTS * SLOTS, COLS), F32),
            pltpu.VMEM((HOSTS, 8, BLOCK), F32),
            pltpu.VMEM((BLOCKS, BLOCK), F32),
            pltpu.VMEM((QUARTERS, 8, COLS), F32),
            pltpu.VMEM((2, 4, 8, 256), F32),
            pltpu.VMEM((2, 8, 8, 256), F32),
            pltpu.VMEM((QUARTERS, 8, COLS), F32),
            pltpu.VMEM((2, HOSTS, BLOCKS, BLOCK), F32),
            pltpu.VMEM((BLOCKS, BLOCK), F32),
            pltpu.VMEM((HOSTS * SLOTS, BLOCK), F32),
            pltpu.VMEM((QUARTERS, WIDTH, COLS), F32),
            pltpu.VMEM((QUARTERS, 2, double, BLOCK), jnp.int16),
            pltpu.VMEM((QUARTERS, 2, double, BLOCK), jnp.int16),
            pltpu.VMEM((QUARTERS, 2, single, BLOCK), jnp.int16),
            pltpu.VMEM((QUARTERS, 2, single, BLOCK), jnp.int16),
            pltpu.VMEM((QUARTERS, 2, single, BLOCK), jnp.int16),
            pltpu.VMEM((8, single, BLOCK), jnp.int16),
            pltpu.VMEM((2 * share, COLS), F32),
            pltpu.VMEM((QUARTERS, BLOCKS + HOSTS, BLOCK), F32),
            pltpu.VMEM((SLOTS, WIDTH), BF16),
            pltpu.VMEM((WIDTH, COLS), BF16),
            dma((2,)),
            dma((13,)),
            dma((13,)),
            dma((24,)),
            dma((24,)),
            dma((7,)),
            dma((7,)),
            dma((6,)),
            dma((6,)),
            dma((14,)),
            dma((14,)),
            dma((28,)),
            dma((28,)),
            dma((3,)),
            dma((3,)),
            dma((16,)),
            dma((16,)),
            dma((8,)),
            dma((8,)),
        ],
        compiler_params=pltpu.CompilerParams(
            collective_id=0, has_side_effects=True, vmem_limit_bytes=62 << 20
        ),
        cost_estimate=pl.CostEstimate(
            flops=13_000_000_000, bytes_accessed=2_000_000, transcendentals=8_400_000
        ),
    )(loader_blocks.reshape(SLOTS, WIDTH), block_counts, block_dest, centroids)
    return numer, weights.reshape(64 * BLOCK)


def solution(mesh):
    in_specs = (P("docs", "cent", None, None), P("docs", "cent"), P("docs", None), P(None, "cent"))
    out_specs = (P("docs", "cent"), P("docs"))
    return jax.shard_map(
        on_device, mesh=mesh, in_specs=in_specs, out_specs=out_specs, check_vma=False
    )
```

```python
import jax
import jax.numpy as jnp
from jax import lax
from jax.experimental import pallas as pl
from jax.experimental.pallas import tpu as pltpu
from jax.sharding import PartitionSpec as P

F32 = jnp.float32
BF16 = jnp.bfloat16

WIDTH = 384
COLS = 512
SLOTS = 512
BLOCK = 128
MOST = 4
HOSTS = 8
BLOCKS = HOSTS * MOST
QUARTERS = 4
SHARPNESS = 25.0
LOG2_E = 1.4426950408889634
STEP = 1.99
DOCS = 65536.0
CENTROIDS = 16384.0


def mod(value, size):
    return lax.rem(value, jnp.int32(size))


def wide(tile):
    return jnp.concatenate([tile] * (COLS // BLOCK), axis=1)


def device(x, y, z, core):
    return (x * 2 + mod(z, 2), (lax.div(z, jnp.int32(2)) * 4 + y) * 2 + core)


def kernel(
    docs_hbm,
    counts_ref,
    dest_ref,
    cents_hbm,
    numer_out,
    weights_out,
    units,
    cents,
    score,
    live_counts,
    live,
    col_acc,
    col_x,
    col_z,
    scale,
    rows,
    doc_row,
    doc_col,
    numer,
    open_out,
    open_in,
    close_out,
    close_in,
    out_z,
    in_z,
    reduced,
    doc_log,
    docs_ref,
    cents_ref,
    load_sem,
    unit_send,
    unit_recv,
    cent_send,
    cent_recv,
    count_send,
    count_recv,
    colx_send,
    colx_recv,
    colz_send,
    colz_recv,
    row_send,
    row_recv,
    log_send,
    log_recv,
    sum_send,
    sum_recv,
    share_send,
    share_recv,
):
    doc_index = lax.axis_index("docs")
    cent_index = lax.axis_index("cent")
    x = lax.div(doc_index, jnp.int32(2))
    lo = mod(doc_index, 2)
    core = mod(cent_index, 2)
    y = mod(lax.div(cent_index, jnp.int32(2)), 4)
    hi = lax.div(cent_index, jnp.int32(8))
    z = hi * 2 + lo
    host = y * 2 + core

    def along_host(step):
        other = mod(host + step, HOSTS)
        return device(x, lax.div(other, jnp.int32(2)), z, mod(other, 2))

    def along_x(step):
        return device(mod(x + step, 4), y, z, core)

    def along_z(step):
        return device(x, y, mod(z + step, 8), core)

    def along_y(step):
        return device(x, mod(y + step, 4), z, core)

    def remote(src, dst, send, recv, target):
        return pltpu.make_async_remote_copy(
            src_ref=src,
            dst_ref=dst,
            send_sem=send,
            recv_sem=recv,
            device_id=target,
            device_id_type=pl.DeviceIdType.MESH,
        )

    to_right, to_left = along_y(1), along_y(3)
    to_twin = device(x, y, z, 1 - core)

    barrier = pltpu.get_barrier_semaphore()
    greeted = [along_z(1), along_z(7)]
    greeted += [along_host(step) for step in range(1, 8)]
    greeted += [along_x(step) for step in range(1, 4)]
    load_docs = pltpu.make_async_copy(docs_hbm, docs_ref, load_sem.at[0])
    load_cents = pltpu.make_async_copy(cents_hbm, cents_ref, load_sem.at[1])
    load_docs.start()
    load_cents.start()
    for other in greeted:
        pl.semaphore_signal(
            barrier, inc=1, device_id=other, device_id_type=pl.DeviceIdType.MESH
        )

    load_docs.wait()
    values = docs_ref[...].astype(F32)
    factor = lax.rsqrt(jnp.mean(values * values, axis=1, keepdims=True) + 1e-06)
    units[host] = (values * factor * WIDTH ** (-0.5)).astype(BF16)
    live_counts[host] = jnp.full((8, BLOCK), counts_ref[0, 0].astype(F32), F32)
    col_acc[...] = jnp.zeros_like(col_acc)

    def score_tiles(which, quarters):
        for quarter in quarters:
            logits = jnp.dot(units[which], cents[quarter], preferred_element_type=F32)
            weights = jnp.exp2((SHARPNESS * LOG2_E) * logits)
            score[quarter, pl.ds(pl.multiple_of(which * SLOTS, SLOTS), SLOTS), :] = weights
            total = col_acc[quarter]
            for slot in range(MOST):
                part = weights[slot * BLOCK : (slot + 1) * BLOCK]
                part = jnp.sum(part.reshape(BLOCK // 8, 8, COLS), axis=0)
                here = jnp.where(live_counts[which] > slot, 1.0, 0.0)
                total = total + part * wide(here)
            col_acc[quarter] = total

    left_y, right_y, far_y = mod(y + 3, 4), mod(y + 1, 4), mod(y + 2, 4)
    first, second, whole = pl.ds(0, SLOTS // 2), pl.ds(SLOTS // 2, SLOTS // 2), pl.ds(0, SLOTS)
    own, from_left, from_right, across = (
        host,
        left_y * 2 + core,
        right_y * 2 + core,
        far_y * 2 + core,
    )
    unit_plan = [
        (own, first, to_right),
        (own, second, to_right),
        (own, first, to_left),
        (own, second, to_left),
        (from_left, first, to_right),
        (from_right, second, to_left),
        (own, whole, to_twin),
        (from_left, first, to_twin),
        (from_left, second, to_twin),
        (from_right, first, to_twin),
        (from_right, second, to_twin),
        (across, first, to_twin),
        (across, second, to_twin),
    ]
    unit_copies = []
    for at, (which, part, target) in enumerate(unit_plan):
        ref = units.at[which, part]
        unit_copies.append(remote(ref, ref, unit_send.at[at], unit_recv.at[at], target))

    chunk = WIDTH // 8
    relay_way, origin_way = lo, 1 - lo
    relay_to, origin_to = along_z(1 + 6 * lo), along_z(7 - 6 * lo)
    relay_quarter = mod(hi + 3 + 2 * lo, QUARTERS)
    other_quarter = mod(hi + 5 - 2 * lo, QUARTERS)
    far_quarter = mod(hi + 2, QUARTERS)
    relays, origins = [], []
    for step in range(12):
        for copies, way, target, blocks in (
            (relays, relay_way, relay_to, (relay_quarter, far_quarter)),
            (origins, origin_way, origin_to, (hi, other_quarter)),
        ):
            line = mod(step + 4 * way, 8) * chunk
            ref = cents.at[blocks[step // 8], pl.ds(pl.multiple_of(line, 16), chunk)]
            at = way * 12 + step
            copies.append(remote(ref, ref, cent_send.at[at], cent_recv.at[at], target))

    count_copies = [
        remote(
            live_counts.at[host],
            live_counts.at[host],
            count_send.at[step - 1],
            count_recv.at[step - 1],
            along_host(step),
        )
        for step in range(1, 8)
    ]

    def take(*numbers):
        for at in numbers:
            unit_copies[at].wait_recv()

    def give(*numbers):
        for at in numbers:
            unit_copies[at].start()

    def relay(*steps):
        for step in steps:
            relays[step].wait_recv()
            relays[step].start()

    def onward(*steps):
        for step in steps:
            origins[step].wait_recv()
            origins[step + 8].start()

    def score_hosts(count, host_of, quarters, unroll):
        def body(at, _):
            score_tiles(host_of(at), quarters)
            return 0

        lax.fori_loop(0, count, body, 0, unroll=unroll)

    def here(at):
        return y * 2 + (core ^ at)

    def sides(at):
        return mod(y + 1 + 2 * at, 4) * 2 + core

    def sides_twin(at):
        return mod(y + 1 + 2 * at, 4) * 2 + 1 - core

    pl.semaphore_wait(barrier, 12)

    for copy in count_copies:
        copy.start()
    give(0, 3, 6)
    load_cents.wait()
    values = cents_ref[...].astype(F32)
    factor = lax.rsqrt(jnp.mean(values * values, axis=0, keepdims=True) + 1e-06)
    cents[hi] = (values * factor * WIDTH ** (-0.5)).astype(BF16)
    for step in range(8):
        origins[step].start()
    give(1, 2)
    score_tiles(host, (hi,))
    relay(0)
    for copy in count_copies:
        copy.wait_recv()
    take(6)
    score_tiles(host ^ 1, (hi,))
    relay(1, 2, 3)
    take(0, 3)
    give(4, 5, 7, 10)
    relay(4, 5)
    onward(0)
    relay(6)
    onward(1)
    relay(7)
    onward(2)
    take(1, 2)
    give(8, 9)
    onward(3)
    score_hosts(2, here, (relay_quarter,), 2)
    relay(8)
    score_hosts(2, sides, (hi, relay_quarter), 2)
    relay(9)
    take(7, 8, 9, 10)
    relay(10)
    score_hosts(2, sides_twin, (hi, relay_quarter), 2)
    for step in range(4, 8):
        origins[step].wait_recv()
    score_hosts(2, here, (other_quarter,), 2)
    relay(11)
    take(4, 5)
    give(11, 12)
    score_hosts(2, sides, (other_quarter,), 2)
    score_hosts(2, sides_twin, (other_quarter,), 2)
    score_tiles(across, (hi, relay_quarter, other_quarter))
    take(11, 12)
    score_tiles(across ^ 1, (hi, relay_quarter, other_quarter))
    for step in range(8, 12):
        origins[step].wait_recv()
    score_hosts(8, lambda at: at, (far_quarter,), 4)

    pending = unit_copies + relays + origins + count_copies

    def mask_rows():
        for which in range(HOSTS):
            for slot in range(MOST):
                at = which * MOST + slot
                live[at : at + 1, :] = jnp.where(live_counts[which, 0:1, :] > slot, 1.0, 0.0)

    def exchange_columns(turn):
        for quarter in range(QUARTERS):
            total = jnp.sum(col_acc[quarter], axis=0, keepdims=True)
            for part in range(2):
                col_x[turn, x, 2 * quarter + part : 2 * quarter + part + 1, :] = total[
                    :, part * 256 : (part + 1) * 256
                ]
        copies = [
            remote(
                col_x.at[turn, x],
                col_x.at[turn, x],
                colx_send.at[turn * 3 + step - 1],
                colx_recv.at[turn * 3 + step - 1],
                along_x(step),
            )
            for step in range(1, 4)
        ]
        for copy in copies:
            copy.start()
        pending.extend(copies)
        if turn == 0:
            mask_rows()
        for copy in copies:
            copy.wait_recv()
        col_z[turn, z] = (col_x[turn, 0] + col_x[turn, 1]) + (col_x[turn, 2] + col_x[turn, 3])
        copies = [
            remote(
                col_z.at[turn, z],
                col_z.at[turn, z],
                colz_send.at[turn * 7 + step - 1],
                colz_recv.at[turn * 7 + step - 1],
                along_z(step),
            )
            for step in range(1, 8)
        ]
        for copy in copies:
            copy.start()
        pending.extend(copies)
        for copy in copies:
            copy.wait_recv()
        total = col_z[turn, 0]
        for other in range(1, 8):
            total = total + col_z[turn, other]
        result = 1.0 / (CENTROIDS * total)
        for quarter in range(QUARTERS):
            line = jnp.concatenate(
                [result[2 * quarter : 2 * quarter + 1], result[2 * quarter + 1 : 2 * quarter + 2]],
                axis=1,
            )
            scale[quarter] = jnp.broadcast_to(line, (8, COLS))

    chunks = 4
    chunk_blocks = BLOCKS // chunks

    def row_pass(turn, half):
        def body(at, _):
            total = None
            for quarter in range(QUARTERS):
                weights = score[quarter, pl.ds(pl.multiple_of(at * BLOCK, BLOCK), BLOCK), :]
                weights = weights.reshape(BLOCK // 8, 8, COLS) * scale[quarter][None]
                weights = weights.reshape(BLOCK, COLS)
                for part in range(COLS // BLOCK):
                    piece = weights[:, part * BLOCK : (part + 1) * BLOCK]
                    total = piece if total is None else total + piece
            rows[turn, host, pl.ds(at, 1), :] = jnp.sum(total.T, axis=0, keepdims=True)
            return 0

        lax.fori_loop(half * chunk_blocks, (half + 1) * chunk_blocks, body, 0, unroll=8)
        ref = rows.at[turn, host, pl.ds(half * chunk_blocks, chunk_blocks)]
        copies = []
        for step in range(1, 8):
            at = (turn * chunks + half) * 7 + step - 1
            copies.append(remote(ref, ref, row_send.at[at], row_recv.at[at], along_host(step)))
        for copy in copies:
            copy.start()
        return copies

    def doc_scales(turn, half, copies):
        pending.extend(copies)
        for copy in copies:
            copy.wait_recv()
        part = slice(half * chunk_blocks, (half + 1) * chunk_blocks)
        total = rows[turn, 0, part, :]
        for other in range(1, HOSTS):
            total = total + rows[turn, other, part, :]
        return part, 1.0 / (DOCS * total)

    exchange_columns(0)

    col_acc[...] = jnp.zeros_like(col_acc)

    def column_body(at, _):
        line = wide(jnp.broadcast_to(doc_row[pl.ds(at, 1), :], (BLOCK, BLOCK)).T)
        for quarter in range(QUARTERS):
            weights = score[quarter, pl.ds(pl.multiple_of(at * BLOCK, BLOCK), BLOCK), :] * line
            col_acc[quarter] += jnp.sum(weights.reshape(BLOCK // 8, 8, COLS), axis=0)
        return 0

    sent = [row_pass(0, half) for half in range(chunks)]
    for half in range(chunks):
        part, doc_scale = doc_scales(0, half, sent[half])
        doc_row[part, :] = doc_scale * live[part, :]
        lax.fori_loop(half * chunk_blocks, (half + 1) * chunk_blocks, column_body, 0, unroll=8)
    exchange_columns(1)

    def spread(at, _):
        line = jnp.broadcast_to(doc_row[pl.ds(at, 1), :], (BLOCK, BLOCK)).T
        doc_col[pl.ds(pl.multiple_of(at * BLOCK, BLOCK), BLOCK), :] = line
        return 0

    share = WIDTH // 8
    tall = 2 * share
    groups = COLS // BLOCK

    def encode(pieces, ref):
        row = lax.broadcasted_iota(jnp.int32, (16, BLOCK), 0)
        powers = jnp.zeros((16, BLOCK), F32)
        for at, values in enumerate(pieces):
            most = jnp.max(jnp.abs(values), axis=0, keepdims=True)
            power = jnp.ceil(jnp.log2(jnp.maximum(most, 1e-30)))
            steps = jnp.round(values * (jnp.exp2(14.0 - power) * STEP))
            steps = steps.astype(jnp.int32).astype(jnp.int16)
            for group in range(groups):
                place = at * groups + group
                lanes = slice(group * BLOCK, (group + 1) * BLOCK)
                ref[place * share : (place + 1) * share, :] = steps[:, lanes]
                powers = jnp.where(row == place, power[:, lanes], powers)
        end = len(pieces) * groups * share
        ref[end : end + 16, :] = powers.astype(jnp.int32).astype(jnp.int16)

    def decode(ref, at, count):
        end = count * groups * share
        powers = ref[end : end + 16, :].astype(jnp.int32).astype(F32)
        factors = jnp.exp2(powers - 14.0) * (1.0 / STEP)
        out = []
        for group in range(groups):
            place = at * groups + group
            steps = ref[place * share : (place + 1) * share, :].astype(jnp.int32).astype(F32)
            out.append(steps * factors[place : place + 1])
        return jnp.concatenate(out, axis=1)

    left_x, right_x, far_x = mod(x + 3, 4), mod(x + 1, 4), mod(x + 2, 4)

    def piece(at, owner, half):
        return numer[at, pl.ds(pl.multiple_of(owner * tall + half * share, 8), share), :]

    ways = ((1, right_x, 1), (3, left_x, 0))

    def sum_copies(at):
        opening, closing = [], []
        for way, (step, _, _) in enumerate(ways):
            place = at * 4 + way * 2
            opening.append(
                remote(
                    open_out.at[at, way],
                    open_in.at[at, way],
                    sum_send.at[place],
                    sum_recv.at[place],
                    along_x(step),
                )
            )
            closing.append(
                remote(
                    close_out.at[at, way],
                    close_in.at[at, way],
                    sum_send.at[place + 1],
                    sum_recv.at[place + 1],
                    along_x(step),
                )
            )
        return opening, closing

    def quarter_of(at):
        return mod(hi + (2, 1, 3, 0)[at], QUARTERS)

    def numerators(at, begin, end):
        quarter = quarter_of(at)
        line = scale[quarter][None]
        total = None
        for which in range(begin, end):
            here = slice(which * SLOTS, (which + 1) * SLOTS)
            factor = wide(doc_col[here, :])
            plan = (factor * score[quarter, here, :]).reshape(SLOTS // 8, 8, COLS) * line
            plan = plan.reshape(SLOTS, COLS).astype(BF16)
            term = lax.dot_general(
                units[which], plan, (((0,), (0,)), ((), ())), preferred_element_type=F32
            )
            total = term if total is None else total + term
        if begin == 0:
            numer[at] = total
        else:
            numer[at] += total

    def share_copy(at, half):
        return remote(
            out_z.at[at, half],
            in_z.at[z],
            share_send.at[at * 2 + half],
            share_recv.at[z],
            device(x, y, quarter_of(at) * 2 + half, core),
        )

    last = QUARTERS - 1
    other_half = pl.ds(pl.multiple_of((1 - lo) * share, 8), share)
    own_half = pl.ds(pl.multiple_of(lo * share, 8), share)
    all_sums = [sum_copies(at) for at in range(QUARTERS)]
    all_shares = [share_copy(at, half) for at in range(last) for half in range(2)]
    all_shares.append(
        remote(
            out_z.at[last, 0],
            in_z.at[z],
            share_send.at[last * 2],
            share_recv.at[z],
            device(x, y, hi * 2 + 1 - lo, core),
        )
    )

    def open_x(at):
        for way, (_, owner, half) in enumerate(ways):
            encode([piece(at, far_x, half), piece(at, owner, 1 - half)], open_out.at[at, way])
            all_sums[at][0][way].start()

    def close_x(at):
        for way, (_, owner, half) in enumerate(ways):
            all_sums[at][0][way].wait_recv()
            total = piece(at, owner, half) + decode(open_in.at[at, way], 0, 2)
            encode([total], close_out.at[at, way])
            all_sums[at][1][way].start()

    def reduce_x(at):
        for way, (_, _, half) in enumerate(ways):
            all_sums[at][1][way].wait_recv()
            total = piece(at, x, half) + decode(open_in.at[at, 1 - way], 1, 2)
            total = total + decode(close_in.at[at, way], 0, 1)
            if at < last:
                encode([total], out_z.at[at, half])
                all_shares[at * 2 + half].start()
            else:
                reduced[half * share : (half + 1) * share, :] = total
        if at == last:
            encode([reduced[other_half, :]], out_z.at[last, 0])
            all_shares[-1].start()

    sent = [row_pass(1, half) for half in range(chunks)]
    for half in range(chunks):
        part, doc_scale = doc_scales(1, half, sent[half])
        doc_log[hi, part, :] = jnp.log(DOCS * doc_scale)
        doc_row[part, :] = DOCS * doc_scale * live[part, :]
        lax.fori_loop(half * chunk_blocks, (half + 1) * chunk_blocks, spread, 0, unroll=8)
        numerators(0, half * HOSTS // chunks, (half + 1) * HOSTS // chunks)
    for which in range(HOSTS):
        doc_log[hi, BLOCKS + which : BLOCKS + which + 1, :] = live_counts[which, 0:1, :]
    log_copies = [
        remote(
            doc_log.at[hi],
            doc_log.at[hi],
            log_send.at[step - 1],
            log_recv.at[step - 1],
            along_z(2 * step),
        )
        for step in range(1, 4)
    ]
    for copy in log_copies:
        copy.start()

    for at in range(QUARTERS):
        if at > 0:
            numerators(at, 0, HOSTS)
        open_x(at)
        if at >= 2:
            close_x(at - 2)
    close_x(2)
    reduce_x(0)

    for copy in log_copies:
        copy.wait()
    counts = jnp.concatenate(
        [doc_log[quarter, BLOCKS : BLOCKS + HOSTS, :] for quarter in range(QUARTERS)], axis=0
    )
    values = jnp.concatenate([doc_log[quarter, 0:BLOCKS, :] for quarter in range(QUARTERS)], axis=0)
    lane = lax.broadcasted_iota(jnp.int32, (32, BLOCK), 1)
    line = lax.broadcasted_iota(jnp.int32, (32, BLOCK), 0)
    owner = lane >> 2
    begin = jnp.sum(jnp.where(line < owner, counts, 0.0), axis=0, keepdims=True)
    held = jnp.sum(jnp.where(line == owner, counts, 0.0), axis=0, keepdims=True)
    slot = (lax.broadcasted_iota(jnp.int32, (1, BLOCK), 1) & 3).astype(F32)
    place = jnp.where(slot < held, begin + slot, -1.0)
    goal = jnp.full((1, BLOCK), -1.0, F32)
    for at in range(64):
        goal = jnp.where(place == float(at), dest_ref[0, at].astype(F32), goal)
    chosen = lax.broadcasted_iota(jnp.int32, (64, BLOCK), 0).astype(F32) == goal
    weights_out[...] = jnp.dot(
        jnp.where(chosen, 1.0, 0.0),
        values,
        precision=lax.Precision.HIGHEST,
        preferred_element_type=F32,
    )

    close_x(3)
    reduce_x(1)
    reduce_x(2)
    reduce_x(3)
    total = reduced[own_half, :]
    for step in range(7, 0, -1):
        other = mod(z + 8 + (1 - 2 * lo) * step, 8)
        remote(
            in_z.at[other], in_z.at[other], share_send.at[0], share_recv.at[other], along_z(1)
        ).wait_recv()
        total = total + decode(in_z.at[other], 0, 1)
    numer_out[...] = total

    for at in range(QUARTERS):
        for copy in all_sums[at][0] + all_sums[at][1]:
            copy.wait_send()
    for copy in pending + all_shares:
        copy.wait_send()


def on_device(loader_blocks, block_counts, block_dest, centroids):
    dma = pltpu.SemaphoreType.DMA
    share = WIDTH // 8
    single = share * (COLS // BLOCK) + 16
    double = 2 * share * (COLS // BLOCK) + 16
    vmem = pl.BlockSpec(memory_space=pltpu.VMEM)
    smem = pl.BlockSpec(memory_space=pltpu.SMEM)
    anywhere = pl.BlockSpec(memory_space=pl.ANY)
    numer, weights = pl.pallas_call(
        kernel,
        out_shape=(
            pltpu.VMEM((share, COLS), F32),
            pltpu.VMEM((64, BLOCK), F32),
        ),
        in_specs=[anywhere, smem, smem, anywhere],
        out_specs=(vmem, vmem),
        scratch_shapes=[
            pltpu.VMEM((HOSTS, SLOTS, WIDTH), BF16),
            pltpu.VMEM((QUARTERS, WIDTH, COLS), BF16),
            pltpu.VMEM((QUARTERS, HOSTS * SLOTS, COLS), F32),
            pltpu.VMEM((HOSTS, 8, BLOCK), F32),
            pltpu.VMEM((BLOCKS, BLOCK), F32),
            pltpu.VMEM((QUARTERS, 8, COLS), F32),
            pltpu.VMEM((2, 4, 8, 256), F32),
            pltpu.VMEM((2, 8, 8, 256), F32),
            pltpu.VMEM((QUARTERS, 8, COLS), F32),
            pltpu.VMEM((2, HOSTS, BLOCKS, BLOCK), F32),
            pltpu.VMEM((BLOCKS, BLOCK), F32),
            pltpu.VMEM((HOSTS * SLOTS, BLOCK), F32),
            pltpu.VMEM((QUARTERS, WIDTH, COLS), F32),
            pltpu.VMEM((QUARTERS, 2, double, BLOCK), jnp.int16),
            pltpu.VMEM((QUARTERS, 2, double, BLOCK), jnp.int16),
            pltpu.VMEM((QUARTERS, 2, single, BLOCK), jnp.int16),
            pltpu.VMEM((QUARTERS, 2, single, BLOCK), jnp.int16),
            pltpu.VMEM((QUARTERS, 2, single, BLOCK), jnp.int16),
            pltpu.VMEM((8, single, BLOCK), jnp.int16),
            pltpu.VMEM((2 * share, COLS), F32),
            pltpu.VMEM((QUARTERS, BLOCKS + HOSTS, BLOCK), F32),
            pltpu.VMEM((SLOTS, WIDTH), BF16),
            pltpu.VMEM((WIDTH, COLS), BF16),
            dma((2,)),
            dma((13,)),
            dma((13,)),
            dma((24,)),
            dma((24,)),
            dma((7,)),
            dma((7,)),
            dma((6,)),
            dma((6,)),
            dma((14,)),
            dma((14,)),
            dma((56,)),
            dma((56,)),
            dma((3,)),
            dma((3,)),
            dma((16,)),
            dma((16,)),
            dma((8,)),
            dma((8,)),
        ],
        compiler_params=pltpu.CompilerParams(
            collective_id=0, has_side_effects=True, vmem_limit_bytes=62 << 20
        ),
        cost_estimate=pl.CostEstimate(
            flops=13_000_000_000, bytes_accessed=2_000_000, transcendentals=8_400_000
        ),
    )(loader_blocks.reshape(SLOTS, WIDTH), block_counts, block_dest, centroids)
    return numer, weights.reshape(64 * BLOCK)


def solution(mesh):
    in_specs = (P("docs", "cent", None, None), P("docs", "cent"), P("docs", None), P(None, "cent"))
    out_specs = (P("docs", "cent"), P("docs"))
    return jax.shard_map(
        on_device, mesh=mesh, in_specs=in_specs, out_specs=out_specs, check_vma=False
    )
```

```python
import jax
import jax.numpy as jnp
from jax import lax
from jax.experimental import pallas as pl
from jax.experimental.pallas import tpu as pltpu
from jax.sharding import PartitionSpec as P

F32 = jnp.float32
BF16 = jnp.bfloat16

WIDTH = 384
COLS = 512
SLOTS = 512
BLOCK = 128
MOST = 4
HOSTS = 8
BLOCKS = HOSTS * MOST
QUARTERS = 4
SHARPNESS = 25.0
LOG2_E = 1.4426950408889634
STEP = 1.99
DOCS = 65536.0
CENTROIDS = 16384.0


def mod(value, size):
    return lax.rem(value, jnp.int32(size))


def wide(tile):
    return jnp.concatenate([tile] * (COLS // BLOCK), axis=1)


def device(x, y, z, core):
    return (x * 2 + mod(z, 2), (lax.div(z, jnp.int32(2)) * 4 + y) * 2 + core)


def kernel(
    docs_hbm,
    counts_ref,
    dest_ref,
    cents_hbm,
    numer_out,
    weights_out,
    units,
    cents,
    score,
    live_counts,
    live,
    col_acc,
    col_x,
    col_z,
    scale,
    rows,
    doc_row,
    doc_col,
    numer,
    open_out,
    open_in,
    close_out,
    close_in,
    out_z,
    in_z,
    reduced,
    doc_log,
    docs_ref,
    cents_ref,
    load_sem,
    unit_send,
    unit_recv,
    cent_send,
    cent_recv,
    count_send,
    count_recv,
    colx_send,
    colx_recv,
    colz_send,
    colz_recv,
    row_send,
    row_recv,
    log_send,
    log_recv,
    sum_send,
    sum_recv,
    share_send,
    share_recv,
):
    doc_index = lax.axis_index("docs")
    cent_index = lax.axis_index("cent")
    x = lax.div(doc_index, jnp.int32(2))
    lo = mod(doc_index, 2)
    core = mod(cent_index, 2)
    y = mod(lax.div(cent_index, jnp.int32(2)), 4)
    hi = lax.div(cent_index, jnp.int32(8))
    z = hi * 2 + lo
    host = y * 2 + core

    def along_host(step):
        other = mod(host + step, HOSTS)
        return device(x, lax.div(other, jnp.int32(2)), z, mod(other, 2))

    def along_x(step):
        return device(mod(x + step, 4), y, z, core)

    def along_z(step):
        return device(x, y, mod(z + step, 8), core)

    def along_y(step):
        return device(x, mod(y + step, 4), z, core)

    def remote(src, dst, send, recv, target):
        return pltpu.make_async_remote_copy(
            src_ref=src,
            dst_ref=dst,
            send_sem=send,
            recv_sem=recv,
            device_id=target,
            device_id_type=pl.DeviceIdType.MESH,
        )

    to_right, to_left = along_y(1), along_y(3)
    to_twin = device(x, y, z, 1 - core)

    barrier = pltpu.get_barrier_semaphore()
    greeted = [along_z(1), along_z(7)]
    greeted += [along_host(step) for step in range(1, 8)]
    greeted += [along_x(step) for step in range(1, 4)]
    load_docs = pltpu.make_async_copy(docs_hbm, docs_ref, load_sem.at[0])
    load_cents = pltpu.make_async_copy(cents_hbm, cents_ref, load_sem.at[1])
    load_docs.start()
    load_cents.start()
    for other in greeted:
        pl.semaphore_signal(
            barrier, inc=1, device_id=other, device_id_type=pl.DeviceIdType.MESH
        )

    load_docs.wait()
    values = docs_ref[...].astype(F32)
    factor = lax.rsqrt(jnp.mean(values * values, axis=1, keepdims=True) + 1e-06)
    units[host] = (values * factor * WIDTH ** (-0.5)).astype(BF16)
    live_counts[host] = jnp.full((8, BLOCK), counts_ref[0, 0].astype(F32), F32)
    col_acc[...] = jnp.zeros_like(col_acc)

    def score_tiles(which, quarters):
        for quarter in quarters:
            logits = jnp.dot(units[which], cents[quarter], preferred_element_type=F32)
            weights = jnp.exp2((SHARPNESS * LOG2_E) * logits)
            score[quarter, pl.ds(pl.multiple_of(which * SLOTS, SLOTS), SLOTS), :] = weights
            total = col_acc[quarter]
            for slot in range(MOST):
                part = weights[slot * BLOCK : (slot + 1) * BLOCK]
                part = jnp.sum(part.reshape(BLOCK // 8, 8, COLS), axis=0)
                here = jnp.where(live_counts[which] > slot, 1.0, 0.0)
                total = total + part * wide(here)
            col_acc[quarter] = total

    left_y, right_y, far_y = mod(y + 3, 4), mod(y + 1, 4), mod(y + 2, 4)
    first, second, whole = pl.ds(0, SLOTS // 2), pl.ds(SLOTS // 2, SLOTS // 2), pl.ds(0, SLOTS)
    own, from_left, from_right, across = (
        host,
        left_y * 2 + core,
        right_y * 2 + core,
        far_y * 2 + core,
    )
    unit_plan = [
        (own, first, to_right),
        (own, second, to_right),
        (own, first, to_left),
        (own, second, to_left),
        (from_left, first, to_right),
        (from_right, second, to_left),
        (own, whole, to_twin),
        (from_left, first, to_twin),
        (from_left, second, to_twin),
        (from_right, first, to_twin),
        (from_right, second, to_twin),
        (across, first, to_twin),
        (across, second, to_twin),
    ]
    unit_copies = []
    for at, (which, part, target) in enumerate(unit_plan):
        ref = units.at[which, part]
        unit_copies.append(remote(ref, ref, unit_send.at[at], unit_recv.at[at], target))

    chunk = WIDTH // 8
    relay_way, origin_way = lo, 1 - lo
    relay_to, origin_to = along_z(1 + 6 * lo), along_z(7 - 6 * lo)
    relay_quarter = mod(hi + 3 + 2 * lo, QUARTERS)
    other_quarter = mod(hi + 5 - 2 * lo, QUARTERS)
    far_quarter = mod(hi + 2, QUARTERS)
    relays, origins = [], []
    for step in range(12):
        for copies, way, target, blocks in (
            (relays, relay_way, relay_to, (relay_quarter, far_quarter)),
            (origins, origin_way, origin_to, (hi, other_quarter)),
        ):
            line = mod(step + 4 * way, 8) * chunk
            ref = cents.at[blocks[step // 8], pl.ds(pl.multiple_of(line, 16), chunk)]
            at = way * 12 + step
            copies.append(remote(ref, ref, cent_send.at[at], cent_recv.at[at], target))

    count_copies = [
        remote(
            live_counts.at[host],
            live_counts.at[host],
            count_send.at[step - 1],
            count_recv.at[step - 1],
            along_host(step),
        )
        for step in (4, 5, 3, 6, 2, 7, 1)
    ]

    def take(*numbers):
        for at in numbers:
            unit_copies[at].wait_recv()

    def give(*numbers):
        for at in numbers:
            unit_copies[at].start()

    def relay(*steps):
        for step in steps:
            relays[step].wait_recv()
            relays[step].start()

    def onward(*steps):
        for step in steps:
            origins[step].wait_recv()
            origins[step + 8].start()

    def score_hosts(count, host_of, quarters, unroll):
        def body(at, _):
            score_tiles(host_of(at), quarters)
            return 0

        lax.fori_loop(0, count, body, 0, unroll=unroll)

    def here(at):
        return y * 2 + (core ^ at)

    def sides(at):
        return mod(y + 1 + 2 * at, 4) * 2 + core

    def sides_twin(at):
        return mod(y + 1 + 2 * at, 4) * 2 + 1 - core

    pl.semaphore_wait(barrier, 12)

    for copy in count_copies:
        copy.start()
    give(0, 3, 6)
    load_cents.wait()
    values = cents_ref[...].astype(F32)
    factor = lax.rsqrt(jnp.mean(values * values, axis=0, keepdims=True) + 1e-06)
    cents[hi] = (values * factor * WIDTH ** (-0.5)).astype(BF16)
    for step in range(8):
        origins[step].start()
    give(1, 2)
    score_tiles(host, (hi,))
    relay(0)
    for copy in count_copies:
        copy.wait_recv()
    take(6)
    score_tiles(host ^ 1, (hi,))
    relay(1, 2, 3)
    take(0, 3)
    give(4, 5, 7, 10)
    relay(4, 5)
    onward(0)
    relay(6)
    onward(1)
    relay(7)
    onward(2)
    take(1, 2)
    give(8, 9)
    onward(3)
    score_hosts(2, here, (relay_quarter,), 2)
    relay(8)
    score_hosts(2, sides, (hi, relay_quarter), 2)
    relay(9)
    take(7, 8, 9, 10)
    relay(10)
    score_hosts(2, sides_twin, (hi, relay_quarter), 2)
    for step in range(4, 8):
        origins[step].wait_recv()
    score_hosts(2, here, (other_quarter,), 2)
    relay(11)
    take(4, 5)
    give(11, 12)
    score_hosts(2, sides, (other_quarter,), 2)
    score_hosts(2, sides_twin, (other_quarter,), 2)
    score_tiles(across, (hi, relay_quarter, other_quarter))
    take(11, 12)
    score_tiles(across ^ 1, (hi, relay_quarter, other_quarter))
    for step in range(8, 12):
        origins[step].wait_recv()
    score_hosts(8, lambda at: at, (far_quarter,), 4)

    pending = unit_copies + relays + origins + count_copies

    def settle():
        while pending:
            pending.pop().wait_send()

    def mask_rows():
        for which in range(HOSTS):
            for slot in range(MOST):
                at = which * MOST + slot
                live[at : at + 1, :] = jnp.where(live_counts[which, 0:1, :] > slot, 1.0, 0.0)

    def exchange_columns(turn):
        for quarter in range(QUARTERS):
            total = jnp.sum(col_acc[quarter], axis=0, keepdims=True)
            for part in range(2):
                col_x[turn, x, 2 * quarter + part : 2 * quarter + part + 1, :] = total[
                    :, part * 256 : (part + 1) * 256
                ]
        copies = [
            remote(
                col_x.at[turn, x],
                col_x.at[turn, x],
                colx_send.at[turn * 3 + step - 1],
                colx_recv.at[turn * 3 + step - 1],
                along_x(step),
            )
            for step in (2, 1, 3)
        ]
        for copy in copies:
            copy.start()
        pending.extend(copies)
        if turn == 0:
            mask_rows()
        for copy in copies:
            copy.wait_recv()
        col_z[turn, z] = (col_x[turn, 0] + col_x[turn, 1]) + (col_x[turn, 2] + col_x[turn, 3])
        copies = [
            remote(
                col_z.at[turn, z],
                col_z.at[turn, z],
                colz_send.at[turn * 7 + step - 1],
                colz_recv.at[turn * 7 + step - 1],
                along_z(step),
            )
            for step in (4, 3, 5, 2, 6, 1, 7)
        ]
        for copy in copies:
            copy.start()
        settle()
        pending.extend(copies)
        for copy in copies:
            copy.wait_recv()
        total = col_z[turn, 0]
        for other in range(1, 8):
            total = total + col_z[turn, other]
        result = 1.0 / (CENTROIDS * total)
        for quarter in range(QUARTERS):
            line = jnp.concatenate(
                [result[2 * quarter : 2 * quarter + 1], result[2 * quarter + 1 : 2 * quarter + 2]],
                axis=1,
            )
            scale[quarter] = jnp.broadcast_to(line, (8, COLS))

    bounds = ((0, 8), (8, 16), (16, 24), (24, 32))
    chunks = len(bounds)

    def row_pass(turn, half):
        def body(at, _):
            total = None
            for quarter in range(QUARTERS):
                weights = score[quarter, pl.ds(pl.multiple_of(at * BLOCK, BLOCK), BLOCK), :]
                weights = weights.reshape(BLOCK // 8, 8, COLS) * scale[quarter][None]
                weights = weights.reshape(BLOCK, COLS)
                for part in range(COLS // BLOCK):
                    piece = weights[:, part * BLOCK : (part + 1) * BLOCK]
                    total = piece if total is None else total + piece
            rows[turn, host, pl.ds(at, 1), :] = jnp.sum(total.T, axis=0, keepdims=True)
            return 0

        lax.fori_loop(*bounds[half], body, 0, unroll=8)
        ref = rows.at[turn, host, pl.ds(bounds[half][0], bounds[half][1] - bounds[half][0])]
        copies = []
        for step in (4, 5, 3, 6, 2, 7, 1):
            at = (turn * chunks + half) * 7 + step - 1
            copies.append(remote(ref, ref, row_send.at[at], row_recv.at[at], along_host(step)))
        for copy in copies:
            copy.start()
        return copies

    def doc_scales(turn, half, copies):
        pending.extend(copies)
        for copy in copies:
            copy.wait_recv()
        part = slice(*bounds[half])
        total = rows[turn, 0, part, :]
        for other in range(1, HOSTS):
            total = total + rows[turn, other, part, :]
        return part, 1.0 / (DOCS * total)

    exchange_columns(0)

    col_acc[...] = jnp.zeros_like(col_acc)

    def column_body(at, _):
        line = wide(jnp.broadcast_to(doc_row[pl.ds(at, 1), :], (BLOCK, BLOCK)).T)
        for quarter in range(QUARTERS):
            weights = score[quarter, pl.ds(pl.multiple_of(at * BLOCK, BLOCK), BLOCK), :] * line
            col_acc[quarter] += jnp.sum(weights.reshape(BLOCK // 8, 8, COLS), axis=0)
        return 0

    sent = [row_pass(0, half) for half in range(chunks)]
    for half in range(chunks):
        part, doc_scale = doc_scales(0, half, sent[half])
        doc_row[part, :] = doc_scale * live[part, :]
        lax.fori_loop(*bounds[half], column_body, 0, unroll=8)
    exchange_columns(1)

    def spread(at, _):
        line = jnp.broadcast_to(doc_row[pl.ds(at, 1), :], (BLOCK, BLOCK)).T
        doc_col[pl.ds(pl.multiple_of(at * BLOCK, BLOCK), BLOCK), :] = line
        return 0

    share = WIDTH // 8
    tall = 2 * share
    groups = COLS // BLOCK

    def encode(pieces, ref):
        row = lax.broadcasted_iota(jnp.int32, (16, BLOCK), 0)
        powers = jnp.zeros((16, BLOCK), F32)
        for at, values in enumerate(pieces):
            most = jnp.max(jnp.abs(values), axis=0, keepdims=True)
            power = jnp.ceil(jnp.log2(jnp.maximum(most, 1e-30)))
            steps = jnp.round(values * (jnp.exp2(14.0 - power) * STEP))
            steps = steps.astype(jnp.int32).astype(jnp.int16)
            for group in range(groups):
                place = at * groups + group
                lanes = slice(group * BLOCK, (group + 1) * BLOCK)
                ref[place * share : (place + 1) * share, :] = steps[:, lanes]
                powers = jnp.where(row == place, power[:, lanes], powers)
        end = len(pieces) * groups * share
        ref[end : end + 16, :] = powers.astype(jnp.int32).astype(jnp.int16)

    def decode(ref, at, count):
        end = count * groups * share
        powers = ref[end : end + 16, :].astype(jnp.int32).astype(F32)
        factors = jnp.exp2(powers - 14.0) * (1.0 / STEP)
        out = []
        for group in range(groups):
            place = at * groups + group
            steps = ref[place * share : (place + 1) * share, :].astype(jnp.int32).astype(F32)
            out.append(steps * factors[place : place + 1])
        return jnp.concatenate(out, axis=1)

    left_x, right_x, far_x = mod(x + 3, 4), mod(x + 1, 4), mod(x + 2, 4)

    def piece(at, owner, half):
        return numer[at, pl.ds(pl.multiple_of(owner * tall + half * share, 8), share), :]

    ways = ((1, right_x, 1), (3, left_x, 0))

    def sum_copies(at):
        opening, closing = [], []
        for way, (step, _, _) in enumerate(ways):
            place = at * 4 + way * 2
            opening.append(
                remote(
                    open_out.at[at, way],
                    open_in.at[at, way],
                    sum_send.at[place],
                    sum_recv.at[place],
                    along_x(step),
                )
            )
            closing.append(
                remote(
                    close_out.at[at, way],
                    close_in.at[at, way],
                    sum_send.at[place + 1],
                    sum_recv.at[place + 1],
                    along_x(step),
                )
            )
        return opening, closing

    def quarter_of(at):
        return mod(hi + (2, 1, 3, 0)[at], QUARTERS)

    def numerators(at, begin, end):
        quarter = quarter_of(at)
        line = scale[quarter][None]
        total = None
        for which in range(begin, end):
            here = slice(which * SLOTS, (which + 1) * SLOTS)
            factor = wide(doc_col[here, :])
            plan = (factor * score[quarter, here, :]).reshape(SLOTS // 8, 8, COLS) * line
            plan = plan.reshape(SLOTS, COLS).astype(BF16)
            term = lax.dot_general(
                units[which], plan, (((0,), (0,)), ((), ())), preferred_element_type=F32
            )
            total = term if total is None else total + term
        if begin == 0:
            numer[at] = total
        else:
            numer[at] += total

    def share_copy(at, half):
        return remote(
            out_z.at[at, half],
            in_z.at[z],
            share_send.at[at * 2 + half],
            share_recv.at[z],
            device(x, y, quarter_of(at) * 2 + half, core),
        )

    last = QUARTERS - 1
    other_half = pl.ds(pl.multiple_of((1 - lo) * share, 8), share)
    own_half = pl.ds(pl.multiple_of(lo * share, 8), share)
    all_sums = [sum_copies(at) for at in range(QUARTERS)]
    all_shares = [share_copy(at, half) for at in range(last) for half in range(2)]
    all_shares.append(
        remote(
            out_z.at[last, 0],
            in_z.at[z],
            share_send.at[last * 2],
            share_recv.at[z],
            device(x, y, hi * 2 + 1 - lo, core),
        )
    )

    def open_x(at):
        for way, (_, owner, half) in enumerate(ways):
            encode([piece(at, far_x, half), piece(at, owner, 1 - half)], open_out.at[at, way])
            all_sums[at][0][way].start()

    def close_x(at):
        for way, (_, owner, half) in enumerate(ways):
            all_sums[at][0][way].wait_recv()
            total = piece(at, owner, half) + decode(open_in.at[at, way], 0, 2)
            encode([total], close_out.at[at, way])
            all_sums[at][1][way].start()

    def reduce_x(at):
        for way, (_, _, half) in enumerate(ways):
            all_sums[at][1][way].wait_recv()
            total = piece(at, x, half) + decode(open_in.at[at, 1 - way], 1, 2)
            total = total + decode(close_in.at[at, way], 0, 1)
            if at < last:
                encode([total], out_z.at[at, half])
                all_shares[at * 2 + half].start()
            else:
                reduced[half * share : (half + 1) * share, :] = total
        if at == last:
            encode([reduced[other_half, :]], out_z.at[last, 0])
            all_shares[-1].start()

    sent = [row_pass(1, half) for half in range(chunks)]
    for half in range(chunks):
        part, doc_scale = doc_scales(1, half, sent[half])
        doc_log[hi, part, :] = jnp.log(DOCS * doc_scale)
        doc_row[part, :] = DOCS * doc_scale * live[part, :]
        lax.fori_loop(*bounds[half], spread, 0, unroll=8)
        numerators(0, bounds[half][0] // MOST, bounds[half][1] // MOST)
    log_copies = []

    def send_logs():
        for which in range(HOSTS):
            doc_log[hi, BLOCKS + which : BLOCKS + which + 1, :] = live_counts[which, 0:1, :]
        copies = [
            remote(
                doc_log.at[hi],
                doc_log.at[hi],
                log_send.at[step - 1],
                log_recv.at[step - 1],
                along_z(2 * step),
            )
            for step in range(1, 4)
        ]
        for copy in copies:
            copy.start()
        log_copies.extend(copies)

    for at in range(QUARTERS):
        if at > 0:
            numerators(at, 0, HOSTS)
        open_x(at)
        if at == 0:
            send_logs()
        if at >= 2:
            close_x(at - 2)
    close_x(2)
    reduce_x(0)
    settle()

    for copy in log_copies:
        copy.wait()
    counts = jnp.concatenate(
        [doc_log[quarter, BLOCKS : BLOCKS + HOSTS, :] for quarter in range(QUARTERS)], axis=0
    )
    values = jnp.concatenate([doc_log[quarter, 0:BLOCKS, :] for quarter in range(QUARTERS)], axis=0)
    lane = lax.broadcasted_iota(jnp.int32, (32, BLOCK), 1)
    line = lax.broadcasted_iota(jnp.int32, (32, BLOCK), 0)
    owner = lane >> 2
    begin = jnp.sum(jnp.where(line < owner, counts, 0.0), axis=0, keepdims=True)
    held = jnp.sum(jnp.where(line == owner, counts, 0.0), axis=0, keepdims=True)
    slot = (lax.broadcasted_iota(jnp.int32, (1, BLOCK), 1) & 3).astype(F32)
    place = jnp.where(slot < held, begin + slot, -1.0)
    goal = jnp.full((1, BLOCK), -1.0, F32)
    for at in range(64):
        goal = jnp.where(place == float(at), dest_ref[0, at].astype(F32), goal)
    chosen = lax.broadcasted_iota(jnp.int32, (64, BLOCK), 0).astype(F32) == goal
    weights_out[...] = jnp.dot(
        jnp.where(chosen, 1.0, 0.0),
        values,
        precision=lax.Precision.HIGHEST,
        preferred_element_type=F32,
    )

    close_x(3)
    reduce_x(1)
    reduce_x(2)
    reduce_x(3)
    total = reduced[own_half, :]
    for step in range(7, 0, -1):
        other = mod(z + 8 + (1 - 2 * lo) * step, 8)
        remote(
            in_z.at[other], in_z.at[other], share_send.at[0], share_recv.at[other], along_z(1)
        ).wait_recv()
        total = total + decode(in_z.at[other], 0, 1)
    numer_out[...] = total

    for at in range(QUARTERS):
        for copy in all_sums[at][0] + all_sums[at][1]:
            copy.wait_send()
    for copy in all_shares:
        copy.wait_send()


def on_device(loader_blocks, block_counts, block_dest, centroids):
    dma = pltpu.SemaphoreType.DMA
    share = WIDTH // 8
    single = share * (COLS // BLOCK) + 16
    double = 2 * share * (COLS // BLOCK) + 16
    vmem = pl.BlockSpec(memory_space=pltpu.VMEM)
    smem = pl.BlockSpec(memory_space=pltpu.SMEM)
    anywhere = pl.BlockSpec(memory_space=pl.ANY)
    numer, weights = pl.pallas_call(
        kernel,
        out_shape=(
            pltpu.VMEM((share, COLS), F32),
            pltpu.VMEM((64, BLOCK), F32),
        ),
        in_specs=[anywhere, smem, smem, anywhere],
        out_specs=(vmem, vmem),
        scratch_shapes=[
            pltpu.VMEM((HOSTS, SLOTS, WIDTH), BF16),
            pltpu.VMEM((QUARTERS, WIDTH, COLS), BF16),
            pltpu.VMEM((QUARTERS, HOSTS * SLOTS, COLS), F32),
            pltpu.VMEM((HOSTS, 8, BLOCK), F32),
            pltpu.VMEM((BLOCKS, BLOCK), F32),
            pltpu.VMEM((QUARTERS, 8, COLS), F32),
            pltpu.VMEM((2, 4, 8, 256), F32),
            pltpu.VMEM((2, 8, 8, 256), F32),
            pltpu.VMEM((QUARTERS, 8, COLS), F32),
            pltpu.VMEM((2, HOSTS, BLOCKS, BLOCK), F32),
            pltpu.VMEM((BLOCKS, BLOCK), F32),
            pltpu.VMEM((HOSTS * SLOTS, BLOCK), F32),
            pltpu.VMEM((QUARTERS, WIDTH, COLS), F32),
            pltpu.VMEM((QUARTERS, 2, double, BLOCK), jnp.int16),
            pltpu.VMEM((QUARTERS, 2, double, BLOCK), jnp.int16),
            pltpu.VMEM((QUARTERS, 2, single, BLOCK), jnp.int16),
            pltpu.VMEM((QUARTERS, 2, single, BLOCK), jnp.int16),
            pltpu.VMEM((QUARTERS, 2, single, BLOCK), jnp.int16),
            pltpu.VMEM((8, single, BLOCK), jnp.int16),
            pltpu.VMEM((2 * share, COLS), F32),
            pltpu.VMEM((QUARTERS, BLOCKS + HOSTS, BLOCK), F32),
            pltpu.VMEM((SLOTS, WIDTH), BF16),
            pltpu.VMEM((WIDTH, COLS), BF16),
            dma((2,)),
            dma((13,)),
            dma((13,)),
            dma((24,)),
            dma((24,)),
            dma((7,)),
            dma((7,)),
            dma((6,)),
            dma((6,)),
            dma((14,)),
            dma((14,)),
            dma((56,)),
            dma((56,)),
            dma((3,)),
            dma((3,)),
            dma((16,)),
            dma((16,)),
            dma((8,)),
            dma((8,)),
        ],
        compiler_params=pltpu.CompilerParams(
            collective_id=0, has_side_effects=True, vmem_limit_bytes=62 << 20
        ),
        cost_estimate=pl.CostEstimate(
            flops=13_000_000_000, bytes_accessed=2_000_000, transcendentals=8_400_000
        ),
    )(loader_blocks.reshape(SLOTS, WIDTH), block_counts, block_dest, centroids)
    return numer, weights.reshape(64 * BLOCK)


def solution(mesh):
    in_specs = (P("docs", "cent", None, None), P("docs", "cent"), P("docs", None), P(None, "cent"))
    out_specs = (P("docs", "cent"), P("docs"))
    return jax.shard_map(
        on_device, mesh=mesh, in_specs=in_specs, out_specs=out_specs, check_vma=False
    )
```
